256 devices in a mesh: seq: 64 (over x, z, core), batch: 4 (over y).
Axes of the slice: x: 4, y: 4, z: 8, core: 2. Of those that a mesh axis runs over, the one named last changes fastest.
Arguments:
- events: bfloat16 [4, 32768, 1, 256], P('batch', 'seq'), may hold values from -6 to 6
- spectral_filter: float32 [2, 32768, 256], P(None, None, 'seq'), may hold values from -6 to 6
- ln_gain: float32 [256], replicated, may hold values from 0.1 to 1.9
- w_in: bfloat16 [64, 1024, 256], P('seq', 'batch'), may hold values from -0.375 to 0.375
- w_out: bfloat16 [64, 1024, 256], P('seq', 'batch'), may hold values from -0.1875 to 0.1875
- gate_weight: bfloat16 [3, 256, 64], replicated, may hold values from -0.375 to 0.375
- gate_table: float32 [3, 16], replicated, may hold values from -4 to 4
- routes: int32 [4, 32768, 1, 1], P('batch', 'seq'), may hold values from 0 to 63; in each aligned block of 512 rows (0 to 511, 512 to 1023, ..., all dimensions but the last counted through in order) at most 16 rows name the same one
- gate_index: int32 [4, 32768, 1, 3], P('batch', 'seq'), may hold values from 0 to 15
Outputs:
- task_out: bfloat16 [3, 4, 32768, 1, 256], P(None, 'batch', 'seq')
The draws below stay inside these ranges and needn't reach their ends.
Inputs may be any that keep to these rules, and one draw needn't show every extreme that they name: `routes`: in each aligned block of 512 rows (the events of one device) no expert is named by more than 16 rows; in some block one expert is named by exactly 16.
All inputs are finite; a program needn't handle non-finite values.
Results may differ from the reference program's by a relative error of at most 0.0072.
Values may be sent and summed in bfloat16 or wider, within the bound.
No kernel may reach another device: no remote copies, remote signals or barrier semaphores. Data moves between devices by JAX's collectives and lax.ppermute only.
A program may use at most 128 MiB of HBM per device.

```python
import math
import jax
import jax.numpy as jnp
import numpy as np
from jax import lax

C = 256
L = 32768
HID = 1024
EXPERTS = 64
TASKS = 3
GATE_ROWS = 16
USERS_DEV = 1
GROUPS = 4
TOK_DEV = 512
CAP = 16


def set_ends(entries, key, smallest, high):
    shape = entries.shape
    spot = [jax.random.randint(jax.random.fold_in(key, axis), (), 0, shape[axis]) for axis in range(len(shape))]
    entries = entries.at[tuple(spot)].set(smallest)
    longest = shape.index(max(shape))
    spot[longest] = (spot[longest] + 1) % shape[longest]
    return entries.at[tuple(spot)].set(high)


def block_levels(rng, extent, pieces, low, top_value):
    factor_of, own = 1.0, jax.random.fold_in(rng, 6)
    for axis_at, shards_of in pieces:
        draws = jnp.exp(jax.random.uniform(jax.random.fold_in(own, axis_at), (shards_of,), jnp.float32, low / len(pieces), top_value / len(pieces)))
        factor_of = factor_of * jnp.repeat(draws, extent[axis_at] // shards_of).reshape([-1 if axis == axis_at else 1 for axis in range(len(extent))])
    return factor_of


def deal_out(stream_key, own, number, rows, number_of, top, bound, slope):
    ranking = jax.random.permutation(stream_key, number_of)
    heavy_load, ordinary = load_shares(number_of, rows * top, bound, slope, True), load_shares(number_of, rows * top, bound, slope, False)
    places = jnp.arange(number_of)

    def named(tallies, rotation):
        used = int((tallies > 0).sum())
        fixed = max(1, used // 4)
        passed = fixed + (places - fixed + rotation * (used - fixed)) % max(1, number_of - fixed)
        return jnp.zeros((number_of,), jnp.int32).at[ranking[jnp.where(places < fixed, places, passed)]].set(jnp.asarray(tallies, jnp.int32))

    tallies = jnp.where(number % 4 == 0, named(heavy_load, number // 4), named(ordinary, number - number // 4 - 1))
    mixed = jax.random.permutation(jax.random.fold_in(own, 3), number_of)
    donor, receiver = mixed[0:number_of // 2 * 2:2], mixed[1:number_of // 2 * 2:2]
    slack = jnp.minimum(tallies[donor] - 1, bound - tallies[receiver]) // 2
    slack = jnp.where((donor == ranking[0]) | (receiver == ranking[0]) | (tallies[receiver] == 0), 0, jnp.maximum(slack, 0))
    passed = jax.random.randint(jax.random.fold_in(own, 4), (number_of // 2,), 0, 1 << 20) % (slack + 1)
    tallies = tallies.at[donor].add(-passed).at[receiver].add(passed)
    items = jnp.searchsorted(jnp.cumsum(tallies), jnp.arange(rows * top), side="right").astype(jnp.int32)
    listing = items.reshape(top, rows).T
    listing = listing[jax.random.permutation(jax.random.fold_in(own, 1), rows)]
    rotation = jax.random.randint(jax.random.fold_in(own, 2), (rows, 1), 0, top)
    return jnp.take_along_axis(listing, (jnp.arange(top)[None, :] + rotation) % top, axis=1)


def load_shares(amount, total, reach, skew, full):
    weights = [(1 << 20) // math.isqrt(grade ** skew) + 1 for grade in range(1, amount + 1)]
    largest = reach if full else min(reach, max(-(-total // amount), total * weights[0] // sum(weights)))
    least = 1 if total - largest >= amount - 1 else 0
    given, spare = [largest] + [least] * (amount - 1), total - largest - least * (amount - 1)
    while spare > 0:
        free = [i for i in range(1, amount) if given[i] < largest] or [i for i in range(1, amount) if given[i] < reach]
        whole, remaining = sum([weights[i] for i in free]), spare
        for i in free:
            addition = min(reach - given[i], max(1, remaining * weights[i] // whole), spare)
            given[i] = given[i] + addition
            spare = spare - addition
    return np.array(given)


def noise(own_key, dims, spread, most, shards=(), kind=jnp.bfloat16):
    drawn = spread * jax.random.normal(own_key, dims, jnp.float32)
    if shards:
        drawn = drawn * block_levels(own_key, dims, shards, -0.22, 0.18)
    return jnp.clip(drawn, -most, most).astype(kind)


def setup_inputs(seed: int = 0) -> dict:
    key_list = jax.random.split(jax.random.key(seed), 10)
    events = noise(key_list[0], (GROUPS, L, USERS_DEV, C), 1.0, 6.0, ((0, 4), (1, 64)))
    spectral_filter = noise(key_list[1], (2, L, C), 1.0, 6.0, ((2, 64),), jnp.float32)
    ln_gain = jnp.clip(1.0 + 0.18 * jax.random.normal(key_list[2], (C,), jnp.float32), 0.1, 1.9)
    w_in = noise(key_list[3], (EXPERTS, HID, C), C ** -0.5, 0.375, ((0, 64), (1, 4)))
    w_out = noise(key_list[4], (EXPERTS, HID, C), HID ** -0.5, 0.1875, ((0, 64), (1, 4)))
    gate_weight = noise(key_list[5], (TASKS, C, EXPERTS), C ** -0.5, 0.375)
    gate_table = noise(key_list[6], (TASKS, GATE_ROWS), 1.0, 4.0, (), jnp.float32)
    routes_keys = jax.random.split(jax.random.fold_in(key_list[7], 1), GROUPS * L * USERS_DEV // TOK_DEV)
    routes_turns = jax.random.permutation(jax.random.fold_in(key_list[7], 3), GROUPS * L * USERS_DEV // TOK_DEV)
    routes = jax.vmap(lambda own, number: deal_out(jax.random.fold_in(key_list[7], 2), own, number, TOK_DEV, EXPERTS, 1, CAP, 2))(routes_keys, routes_turns).reshape((GROUPS, L, USERS_DEV, 1))
    gate_index = set_ends(jax.random.randint(key_list[8], (GROUPS, L, USERS_DEV, TASKS), 0, GATE_ROWS), jax.random.fold_in(key_list[8], 1), 0, GATE_ROWS - 1).astype(jnp.int32)
    return dict(events=events, spectral_filter=spectral_filter, ln_gain=ln_gain, w_in=w_in, w_out=w_out, gate_weight=gate_weight, gate_table=gate_table, routes=routes, gate_index=gate_index)


def layer_norm(summed, gain_vec):
    centre = lax.optimization_barrier(jnp.mean(summed, -1, keepdims=True))
    spread_sq = lax.optimization_barrier(jnp.mean(jnp.square(summed - centre), -1, keepdims=True))
    return ((summed - centre) * lax.rsqrt(spread_sq + 1e-05) * gain_vec).astype(jnp.bfloat16)

def reference(events, spectral_filter, ln_gain, w_in, w_out, gate_weight, gate_table, routes, gate_index):
    filter_full = lax.complex(spectral_filter[0], spectral_filter[1])

    def filter_one(sequence):
        values = sequence.astype(jnp.float32)
        spectrum = jnp.fft.fft(values, axis=0)
        filtered = jnp.real(jnp.fft.ifft(spectrum * filter_full, axis=0)).astype(jnp.float32)
        return (values + filtered).astype(jnp.bfloat16)
    histories = jnp.transpose(events, (0, 2, 1, 3)).reshape(GROUPS * USERS_DEV, L, C)
    summed = lax.map(filter_one, histories).reshape(GROUPS, USERS_DEV, L, C).transpose(0, 2, 1, 3)
    normed = layer_norm(summed.astype(jnp.float32), ln_gain).reshape(-1, C)
    expert_ids = routes.reshape(-1).astype(jnp.int32)
    row_total = expert_ids.shape[0]
    sort_order = jnp.argsort(expert_ids, stable=True).astype(jnp.int32)
    block_rows = math.gcd(row_total, 512)
    sorted_rows = normed[sort_order].reshape(-1, block_rows, C)
    sorted_ids = expert_ids[sort_order].reshape(-1, block_rows)
    gate_cols = gate_weight.transpose(1, 0, 2).reshape(C, TASKS * EXPERTS)

    def run_block(pair):
        rows, block_ids = pair

        def apply_one(expert, current):
            hidden = jnp.maximum(jnp.dot(rows, w_in[expert].T, preferred_element_type=jnp.float32), 0.0).astype(jnp.bfloat16)
            output = jnp.dot(hidden, w_out[expert], preferred_element_type=jnp.float32)
            return jnp.where((block_ids == expert)[:, None], output, current)
        initial = jnp.zeros((block_rows, C), jnp.float32)
        expert_out = lax.fori_loop(block_ids[0], block_ids[-1] + 1, apply_one, initial).astype(jnp.bfloat16)
        scores = jnp.dot(rows, gate_cols, preferred_element_type=jnp.float32).reshape(block_rows, TASKS, EXPERTS)
        chosen = jnp.take_along_axis(scores, block_ids[:, None, None], axis=2)[:, :, 0].astype(jnp.bfloat16)
        return (expert_out, chosen)
    out_sorted, chosen_sorted = lax.map(run_block, (sorted_rows, sorted_ids))
    expert_rows = jnp.zeros((row_total, C), jnp.bfloat16).at[sort_order].set(out_sorted.reshape(row_total, C))
    chosen = jnp.zeros((row_total, TASKS), jnp.bfloat16).at[sort_order].set(chosen_sorted.reshape(row_total, TASKS))
    lookup = gate_index.reshape(row_total, TASKS)
    table_bias = gate_table[jnp.arange(TASKS, dtype=jnp.int32)[None, :], lookup]
    gate_vals = jax.nn.sigmoid(chosen.astype(jnp.float32) + table_bias)
    task_out = (gate_vals.T[:, :, None] * expert_rows.astype(jnp.float32)[None]).astype(jnp.bfloat16)
    return task_out.reshape(TASKS, GROUPS, L, USERS_DEV, C)
```

```python
import functools

import jax
import jax.numpy as jnp
import ml_dtypes
import numpy as np
from jax import lax
from jax.experimental import pallas as pl
from jax.experimental.pallas import tpu as pltpu
from jax.sharding import PartitionSpec as P

EXPERTS = 64
TASKS = 3
CAP = 16
ROWS = 256
COLS = 128
LENGTH = ROWS * COLS
BF16 = jnp.bfloat16
F32 = jnp.float32

NN = (((1,), (0,)), ((), ()))
NT = (((1,), (1,)), ((), ()))


def dot(a, b, dims):
    return lax.dot_general(a, b, dims, preferred_element_type=F32)


def split(x):
    hi = x.astype(BF16)
    return hi, (x - hi.astype(F32)).astype(BF16)


def np_split(x):
    hi = x.astype(ml_dtypes.bfloat16)
    return hi, (x - hi.astype(np.float64)).astype(ml_dtypes.bfloat16)


def cos_sin(rows, cols, points):
    angle = 2.0 * np.pi * (np.outer(np.arange(rows), np.arange(cols)) % points) / points
    return np.cos(angle), np.sin(angle)


def tables():
    cos_r, sin_r = cos_sin(ROWS, ROWS, ROWS)
    cos_c, sin_c = cos_sin(COLS, COLS, COLS)
    tw_cos, tw_sin = cos_sin(ROWS, COLS, LENGTH)
    first = np.stack(np_split(np.concatenate([cos_r, -sin_r], 0)))
    second = np.stack(np_split(np.block([[cos_c, sin_c], [-sin_c, cos_c]])))
    third = np.stack(np_split(np.block([[cos_c, -sin_c], [sin_c, cos_c]])))
    fourth = np.stack(np_split(np.concatenate([cos_r, -sin_r], 1) / LENGTH))
    turn = np.stack([tw_cos, tw_sin]).astype(np.float32)
    turn_back = np.stack([tw_cos.T, tw_sin.T]).astype(np.float32)
    return first, second, third, fourth, turn, turn_back


def join_lanes(wide, out_ref):
    for half in range(2):
        out_ref[:, half * 128 : (half + 1) * 128] = wide[half].astype(BF16)


def deinterleave(x_ref, wide):
    for half in range(2):
        wide[half] = x_ref[:, half * 128 : (half + 1) * 128].astype(F32)
    return jnp.concatenate(
        [wide[half, pl.ds(odd, 256, stride=2), :] for odd in range(2) for half in range(2)], 1
    )


def prep_kernel(ev_ref, out_ref, mid, wide):
    for pb in range(4):
        mid[...] = ev_ref[pb * 128 : (pb + 1) * 128, :].astype(F32).T
        for ch in range(4):
            chp, chl = ch // 2, ch % 2
            wide[chl, pl.ds(pb * 2 + chp, 64, stride=8), :] = mid[pl.ds(ch, 64, stride=4), :]
    join_lanes(wide, out_ref)


def filter_kernel(
    x_ref, spec_ref, first_ref, second_ref, third_ref, fourth_ref, turn_ref, back_ref,
    out_ref, wide, sums,
):
    sig = deinterleave(x_ref, wide)
    sig16 = sig.astype(BF16)
    spec1 = dot(first_ref[0], sig16, NN) + dot(first_ref[1], sig16, NN)
    tcos, tsin = turn_ref[0], turn_ref[1]
    turned = []
    for ch in range(4):
        re = spec1[:256, ch * 128 : (ch + 1) * 128]
        im = spec1[256:, ch * 128 : (ch + 1) * 128]
        turned.append(jnp.concatenate([re * tcos + im * tsin, im * tcos - re * tsin], 1))
    t_hi, t_lo = split(jnp.concatenate(turned, 0))
    spec2 = (
        dot(second_ref[0], t_hi, NT) + dot(second_ref[0], t_lo, NT) + dot(second_ref[1], t_hi, NT)
    )
    prods = []
    for ch in range(4):
        fr = jnp.concatenate(
            [spec_ref[0, pl.ds(4 * h + ch, 128, stride=8), :] for h in range(2)], 1
        )
        fi = jnp.concatenate(
            [spec_ref[1, pl.ds(4 * h + ch, 128, stride=8), :] for h in range(2)], 1
        )
        zr = spec2[:128, ch * 256 : (ch + 1) * 256]
        zi = spec2[128:, ch * 256 : (ch + 1) * 256]
        prods.append(jnp.concatenate([zr * fr - zi * fi, zr * fi + zi * fr], 0))
    p_hi, p_lo = split(jnp.concatenate(prods, 1))
    back = dot(third_ref[0], p_hi, NN) + dot(third_ref[0], p_lo, NN) + dot(third_ref[1], p_hi, NN)
    bcos, bsin = back_ref[0], back_ref[1]
    turned = []
    for ch in range(4):
        re = back[:128, ch * 256 : (ch + 1) * 256]
        im = back[128:, ch * 256 : (ch + 1) * 256]
        turned.append(jnp.concatenate([re * bcos - im * bsin, im * bcos + re * bsin], 1))
    v_hi, v_lo = split(jnp.concatenate(turned, 0))
    filtered = (
        dot(fourth_ref[0], v_hi, NT) + dot(fourth_ref[0], v_lo, NT) + dot(fourth_ref[1], v_hi, NT)
    )
    summed = sig + filtered
    for ch in range(4):
        sums[ch] = summed[:, ch * 128 : (ch + 1) * 128]
    for pb in range(4):
        for ch in range(4):
            wide[pb % 2, pl.ds(ch * 2 + pb // 2, 64, stride=8), :] = sums[
                ch, pl.ds(pb, 64, stride=4), :
            ]
    join_lanes(wide, out_ref)


def route_kernel(routes_ref, put_ref, take_ref):
    experts = routes_ref[...]
    onehot = (lax.broadcasted_iota(jnp.int32, (EXPERTS, 512), 0) == experts).astype(F32)
    before = lax.broadcasted_iota(jnp.int32, (512, 512), 0) < lax.broadcasted_iota(
        jnp.int32, (512, 512), 1
    )
    earlier = dot(onehot.astype(BF16), before.astype(F32).astype(BF16), NN)
    rank = jnp.sum(earlier * onehot, 0, keepdims=True)
    slot = experts.astype(F32) * CAP + rank
    put_ref[...] = (
        lax.broadcasted_iota(jnp.int32, (EXPERTS * CAP, 512), 0) == slot.astype(jnp.int32)
    ).astype(F32).astype(BF16)
    slot_col = jnp.broadcast_to(slot, (128, 512)).T[:, 0:1].astype(jnp.int32)
    take_ref[...] = (
        lax.broadcasted_iota(jnp.int32, (512, EXPERTS * CAP), 1) == slot_col
    ).astype(F32).astype(BF16)


def norm_kernel(x_ref, gain_ref, put_ref, out_ref, normed_ref, wide):
    vals = deinterleave(x_ref, wide)
    centre = jnp.sum(vals, 0, keepdims=True) * (1.0 / 256)
    off = vals - centre
    spread = jnp.sum(off * off, 0, keepdims=True) * (1.0 / 256)
    normed = (off * lax.rsqrt(spread + 1e-05) * gain_ref[...]).astype(BF16)
    normed_ref[...] = normed
    out_ref[...] = dot(put_ref[...], normed, NT).astype(BF16)


def gate_kernel(normed_ref, weight_ref, routes_ref, index_ref, table_ref, out_ref):
    scores = dot(weight_ref[...], normed_ref[...], NN)
    mask = lax.broadcasted_iota(jnp.int32, (EXPERTS, 512), 0) == routes_ref[...]
    rows = []
    for t in range(TASKS):
        part = scores[t * EXPERTS : (t + 1) * EXPERTS]
        chosen = jnp.sum(jnp.where(mask, part, 0.0), 0, keepdims=True).astype(BF16).astype(F32)
        idx = index_ref[t : t + 1, :]
        bias = jnp.zeros((1, 512), F32)
        for r in range(table_ref.shape[1]):
            bias = jnp.where(idx == r, table_ref[t, r], bias)
        rows.append(jax.nn.sigmoid(chosen + bias))
    rows.append(jnp.zeros((128 - TASKS, 512), F32))
    out_ref[...] = jnp.concatenate(rows, 0).T


def ffn_kernel(x_ref, weights_ref, out_ref):
    w_in = weights_ref[:, 0].reshape(1024, 256)
    w_out = weights_ref[:, 1].reshape(1024, 256)
    hidden = jnp.maximum(dot(x_ref[...], w_in, NT), 0.0).astype(BF16)
    out_ref[...] = dot(hidden, w_out, NN).astype(BF16)


def final_kernel(slots_ref, take_ref, gate_ref, out_ref):
    rows = dot(take_ref[...], slots_ref[...], NN)
    for t in range(TASKS):
        out_ref[t] = (gate_ref[:, t : t + 1] * rows).astype(BF16)


def call(kernel, outs, *args, scratch=(), smem=(), flops=0, name=None):
    specs = [
        pl.BlockSpec(memory_space=pltpu.SMEM if i in smem else pltpu.VMEM)
        for i in range(len(args))
    ]
    many = isinstance(outs, (tuple, list))
    return pl.pallas_call(
        kernel,
        out_shape=outs,
        in_specs=specs,
        out_specs=[pl.BlockSpec(memory_space=pltpu.VMEM)] * len(outs)
        if many
        else pl.BlockSpec(memory_space=pltpu.VMEM),
        scratch_shapes=list(scratch),
        compiler_params=pltpu.CompilerParams(vmem_limit_bytes=32 * 2**20),
        cost_estimate=pl.CostEstimate(flops=flops, bytes_accessed=2**20, transcendentals=0),
        name=name,
    )(*args)


def shape(dims, dtype):
    return jax.ShapeDtypeStruct(dims, dtype)


def swap(values, rows):
    lanes = values.shape[-1]
    chunks = values.reshape(64, rows, lanes)
    return lax.all_to_all(chunks, "seq", split_axis=0, concat_axis=0, tiled=True).reshape(
        64 * rows, lanes
    )


def on_device(
    events, spectral_filter, ln_gain, w_in, w_out, gate_weight, gate_table, routes, gate_index
):
    big = pltpu.VMEM
    chunks = call(
        prep_kernel, shape((512, 256), BF16), events.reshape(512, 256),
        scratch=[big((256, 128), F32), big((2, 512, 128), F32)], name="prep",
    )
    arrived = swap(chunks, 8)
    weights = lax.all_gather(jnp.stack([w_in[0], w_out[0]]), "batch", axis=0, tiled=False)
    route_row = routes.reshape(1, 512)
    put, take = call(
        route_kernel, [shape((1024, 512), BF16), shape((512, 1024), BF16)], route_row, name="route"
    )
    spec = spectral_filter.reshape(2, 256, 128, 4).transpose(0, 1, 3, 2).reshape(2, 1024, 128)
    consts = [jnp.asarray(t) for t in tables()]
    sums = call(
        filter_kernel, shape((512, 256), BF16), arrived, spec, *consts,
        scratch=[big((2, 512, 128), F32), big((4, 256, 128), F32)], name="filter", flops=2 * 10**9,
    )
    returned = swap(sums, 8)
    outgoing, normed = call(
        norm_kernel, [shape((1024, 256), BF16), shape((256, 512), BF16)],
        returned, ln_gain.reshape(256, 1), put, scratch=[big((2, 512, 128), F32)], name="norm",
    )
    slots_in = swap(outgoing, 16)
    gates = call(
        gate_kernel, shape((512, 128), F32), normed,
        gate_weight.transpose(0, 2, 1).reshape(192, 256), route_row,
        gate_index.reshape(512, 3).T, gate_table, smem=(4,), name="gate",
    )
    slots_out = call(ffn_kernel, shape((1024, 256), BF16), slots_in, weights, name="ffn", flops=10**9)
    results = swap(slots_out, 16)
    out = call(final_kernel, shape((3, 512, 256), BF16), results, take, gates, name="final")
    return out.reshape(TASKS, 1, 512, 1, 256)


def solution(mesh):
    in_specs = (
        P("batch", "seq", None, None),
        P(None, None, "seq"),
        P(),
        P("seq", "batch", None),
        P("seq", "batch", None),
        P(),
        P(),
        P("batch", "seq", None, None),
        P("batch", "seq", None, None),
    )
    out_specs = P(None, "batch", "seq", None, None)
    return jax.shard_map(
        on_device, mesh=mesh, in_specs=in_specs, out_specs=out_specs, check_vma=False
    )
```

```python
import functools

import jax
import jax.numpy as jnp
import ml_dtypes
import numpy as np
from jax import lax
from jax.experimental import pallas as pl
from jax.experimental.pallas import tpu as pltpu
from jax.sharding import PartitionSpec as P

EXPERTS = 64
TASKS = 3
CAP = 16
ROWS = 256
COLS = 128
LENGTH = ROWS * COLS
BF16 = jnp.bfloat16
F32 = jnp.float32

NN = (((1,), (0,)), ((), ()))
NT = (((1,), (1,)), ((), ()))


def dot(a, b, dims):
    return lax.dot_general(a, b, dims, preferred_element_type=F32)


def split(x):
    hi = x.astype(BF16)
    return hi, (x - hi.astype(F32)).astype(BF16)


def np_split(x):
    hi = x.astype(ml_dtypes.bfloat16)
    return hi, (x - hi.astype(np.float64)).astype(ml_dtypes.bfloat16)


def cos_sin(rows, cols, points):
    angle = 2.0 * np.pi * (np.outer(np.arange(rows), np.arange(cols)) % points) / points
    return np.cos(angle), np.sin(angle)


def tables():
    cos_r, sin_r = cos_sin(ROWS, ROWS, ROWS)
    cos_c, sin_c = cos_sin(COLS, COLS, COLS)
    tw_cos, tw_sin = cos_sin(ROWS, COLS, LENGTH)
    first = np.concatenate([cos_r, -sin_r], 0)
    second = np.block([[cos_c, sin_c], [-sin_c, cos_c]])
    factors = np.concatenate([part for m in (first, second) for part in np_split(m)])
    turns = [t[i : i + 128] for t in (tw_cos, tw_sin) for i in (0, 128)]
    return factors, np.stack(turns).astype(np.float32)


def join_lanes(wide, out_ref):
    for half in range(2):
        out_ref[:, half * 128 : (half + 1) * 128] = wide[half].astype(BF16)


def deinterleave(x_ref, wide):
    for half in range(2):
        wide[half] = x_ref[:, half * 128 : (half + 1) * 128].astype(F32)
    return jnp.concatenate(
        [wide[half, pl.ds(odd, 256, stride=2), :] for odd in range(2) for half in range(2)], 1
    )


def prep_kernel(ev_ref, out_ref, landed, mid, wide, sems):
    copies = [
        pltpu.make_async_copy(
            ev_ref.at[pl.ds(pb * 128, 128)], landed.at[pl.ds(pb * 128, 128)], sems.at[pb]
        )
        for pb in range(4)
    ]
    for copy in copies:
        copy.start()
    for pb in range(4):
        copies[pb].wait()
        mid[...] = landed[pb * 128 : (pb + 1) * 128, :].astype(F32).T
        for ch in range(4):
            chp, chl = ch // 2, ch % 2
            wide[chl, pl.ds(pb * 2 + chp, 64, stride=8), :] = mid[pl.ds(ch, 64, stride=4), :]
    join_lanes(wide, out_ref)


def filter_kernel(x_ref, spec_ref, factor_ref, turn_ref, out_ref, wide, sums):
    first = factor_ref[0:512], factor_ref[512:1024]
    second = factor_ref[1024:1280], factor_ref[1280:1536]
    fourth = [jnp.concatenate([part[:256], part[256:]], 1) for part in first]
    sig = deinterleave(x_ref, wide)
    sig16 = sig.astype(BF16)
    spec1 = dot(first[0], sig16, NN) + dot(first[1], sig16, NN)
    tcos, tsin = [jnp.concatenate([turn_ref[i], turn_ref[i + 1]], 0) for i in (0, 2)]
    turned = []
    for ch in range(4):
        re = spec1[:256, ch * 128 : (ch + 1) * 128]
        im = spec1[256:, ch * 128 : (ch + 1) * 128]
        turned.append(jnp.concatenate([re * tcos + im * tsin, im * tcos - re * tsin], 1))
    t_hi, t_lo = split(jnp.concatenate(turned, 0))
    spec2 = (
        dot(second[0], t_hi, NT) + dot(second[0], t_lo, NT) + dot(second[1], t_hi, NT)
    )
    prods = []
    for ch in range(4):
        fr = spec_ref[0, :, ch * 256 : (ch + 1) * 256]
        fi = spec_ref[1, :, ch * 256 : (ch + 1) * 256]
        zr = spec2[:128, ch * 256 : (ch + 1) * 256]
        zi = spec2[128:, ch * 256 : (ch + 1) * 256]
        prods.append(jnp.concatenate([zr * fi + zi * fr, zr * fr - zi * fi], 0))
    p_hi, p_lo = split(jnp.concatenate(prods, 1))
    back = dot(second[0], p_hi, NN) + dot(second[0], p_lo, NN) + dot(second[1], p_hi, NN)
    bcos, bsin = [jnp.concatenate([turn_ref[i].T, turn_ref[i + 1].T], 1) for i in (0, 2)]
    turned = []
    for ch in range(4):
        im = back[:128, ch * 256 : (ch + 1) * 256]
        re = back[128:, ch * 256 : (ch + 1) * 256]
        turned.append(jnp.concatenate([re * bcos - im * bsin, im * bcos + re * bsin], 1))
    v_hi, v_lo = split(jnp.concatenate(turned, 0))
    filtered = (
        dot(fourth[0], v_hi, NT) + dot(fourth[0], v_lo, NT) + dot(fourth[1], v_hi, NT)
    )
    summed = sig + filtered * (1.0 / LENGTH)
    for ch in range(4):
        sums[ch] = summed[:, ch * 128 : (ch + 1) * 128]
    for pb in range(4):
        for ch in range(4):
            wide[pb % 2, pl.ds(ch * 2 + pb // 2, 64, stride=8), :] = sums[
                ch, pl.ds(pb, 64, stride=4), :
            ]
    join_lanes(wide, out_ref)


def ready_kernel(
    after_ref, spec_ref, factor_ref, turn_ref, spec_out, factor_out, turn_out, raw, sems
):
    copies = [
        pltpu.make_async_copy(src, dst, sems.at[i])
        for i, (src, dst) in enumerate(
            ((spec_ref, raw), (factor_ref, factor_out), (turn_ref, turn_out))
        )
    ]
    for copy in copies:
        copy.start()
    copies[0].wait()
    for part in range(2):
        for ch in range(4):
            for half in range(2):
                at = ch * 256 + half * 128
                spec_out[part, :, at : at + 128] = raw[part, pl.ds(4 * half + ch, 128, stride=8), :]
    copies[1].wait()
    copies[2].wait()


def route_kernel(after_ref, routes_ref, put_ref, slot_ref):
    experts = routes_ref[...]
    onehot = (lax.broadcasted_iota(jnp.int32, (EXPERTS, 512), 0) == experts).astype(F32)
    before = lax.broadcasted_iota(jnp.int32, (512, 512), 0) < lax.broadcasted_iota(
        jnp.int32, (512, 512), 1
    )
    earlier = dot(onehot.astype(BF16), before.astype(F32).astype(BF16), NN)
    rank = jnp.sum(earlier * onehot, 0, keepdims=True)
    slot = experts.astype(F32) * CAP + rank
    put_ref[...] = (
        lax.broadcasted_iota(jnp.int32, (EXPERTS * CAP, 512), 0) == slot.astype(jnp.int32)
    ).astype(F32).astype(BF16)
    slot_ref[...] = jnp.broadcast_to(slot, (8, 512))


def norm_kernel(x_ref, gain_ref, put_ref, out_ref, normed_ref, wide):
    vals = deinterleave(x_ref, wide)
    centre = jnp.sum(vals, 0, keepdims=True) * (1.0 / 256)
    off = vals - centre
    spread = jnp.sum(off * off, 0, keepdims=True) * (1.0 / 256)
    normed = (off * lax.rsqrt(spread + 1e-05) * gain_ref[...]).astype(BF16)
    normed_ref[...] = normed
    out_ref[...] = dot(put_ref[...], normed, NT).astype(BF16)


def gate_kernel(
    after_ref, normed_ref, weight_ref, routes_ref, index_ref, table_ref, slot_ref, out_ref, take_ref
):
    slot_col = jnp.broadcast_to(slot_ref[0:1, :], (128, 512)).T[:, 0:1].astype(jnp.int32)
    take_ref[...] = (
        lax.broadcasted_iota(jnp.int32, (512, EXPERTS * CAP), 1) == slot_col
    ).astype(F32).astype(BF16)
    scores = dot(weight_ref[...], normed_ref[...], NN)
    mask = lax.broadcasted_iota(jnp.int32, (EXPERTS, 512), 0) == routes_ref[...]
    rows = []
    for t in range(TASKS):
        part = scores[t * EXPERTS : (t + 1) * EXPERTS]
        chosen = jnp.sum(jnp.where(mask, part, 0.0), 0, keepdims=True).astype(BF16).astype(F32)
        idx = index_ref[t : t + 1, :]
        bias = jnp.zeros((1, 512), F32)
        for r in range(table_ref.shape[1]):
            bias = jnp.where(idx == r, table_ref[t, r], bias)
        rows.append(jax.nn.sigmoid(chosen + bias))
    rows.append(jnp.zeros((128 - TASKS, 512), F32))
    out_ref[...] = jnp.concatenate(rows, 0).T


def ffn_kernel(x_ref, own_ref, one_ref, two_ref, three_ref, out_ref):
    x = x_ref[...]
    total = None
    for part in (own_ref, one_ref, two_ref, three_ref):
        hidden = jnp.maximum(dot(x, part[0], NT), 0.0).astype(BF16)
        term = dot(hidden, part[1], NN)
        total = term if total is None else total + term
    out_ref[...] = total.astype(BF16)


def final_kernel(slots_ref, take_ref, gate_ref, out_ref):
    rows = dot(take_ref[...], slots_ref[...], NN)
    for t in range(TASKS):
        out_ref[t] = (gate_ref[:, t : t + 1] * rows).astype(BF16)


def call(kernel, outs, *args, scratch=(), smem=(), far=(), flops=0, name=None):
    specs = [
        pl.BlockSpec(memory_space=pltpu.SMEM if i in smem else pl.ANY if i in far else pltpu.VMEM)
        for i in range(len(args))
    ]
    many = isinstance(outs, (tuple, list))
    return pl.pallas_call(
        kernel,
        out_shape=outs,
        in_specs=specs,
        out_specs=[pl.BlockSpec(memory_space=pltpu.VMEM)] * len(outs)
        if many
        else pl.BlockSpec(memory_space=pltpu.VMEM),
        scratch_shapes=list(scratch),
        compiler_params=pltpu.CompilerParams(vmem_limit_bytes=32 * 2**20),
        cost_estimate=pl.CostEstimate(flops=flops, bytes_accessed=2**20, transcendentals=0),
        name=name,
    )(*args)


def shape(dims, dtype):
    return jax.ShapeDtypeStruct(dims, dtype)


def swap(values, rows):
    lanes = values.shape[-1]
    chunks = values.reshape(64, rows, lanes)
    return lax.all_to_all(chunks, "seq", split_axis=0, concat_axis=0, tiled=True).reshape(
        64 * rows, lanes
    )


def on_device(
    events, spectral_filter, ln_gain, w_in, w_out, gate_weight, gate_table, routes, gate_index
):
    big = pltpu.VMEM
    chunks = call(
        prep_kernel, shape((512, 256), BF16), events.reshape(512, 256),
        far=(0,), name="prep",
        scratch=[
            big((512, 256), BF16), big((256, 128), F32), big((2, 512, 128), F32),
            pltpu.SemaphoreType.DMA((4,)),
        ],
    )
    arrived = swap(chunks, 8)
    own = jnp.stack([w_in[0], w_out[0]])
    weights = [own] + [
        lax.ppermute(own, "batch", [(i, (i + d) % 4) for i in range(4)]) for d in (1, 3, 2)
    ]
    route_row = routes.reshape(1, 512)
    spec = spectral_filter.reshape(2, 256, 128, 4).transpose(0, 1, 3, 2).reshape(2, 1024, 128)
    factors, turns = [jnp.asarray(t) for t in tables()]
    spec, factors, turns = call(
        ready_kernel,
        [shape((2, 128, 1024), F32), shape(factors.shape, BF16), shape(turns.shape, F32)],
        chunks, spec, factors, turns, far=(0, 1, 2, 3), name="ready",
        scratch=[big((2, 1024, 128), F32), pltpu.SemaphoreType.DMA((3,))], flops=2 * 10**9,
    )
    sums = call(
        filter_kernel, shape((512, 256), BF16), arrived, spec, factors, turns,
        scratch=[big((2, 512, 128), F32), big((4, 256, 128), F32)], name="filter", flops=2 * 10**9,
    )
    returned = swap(sums, 8)
    put, slot = call(
        route_kernel, [shape((1024, 512), BF16), shape((8, 512), F32)], sums, route_row,
        far=(0,), name="route", flops=2 * 10**9,
    )
    outgoing, normed = call(
        norm_kernel, [shape((1024, 256), BF16), shape((256, 512), BF16)],
        returned, ln_gain.reshape(256, 1), put, scratch=[big((2, 512, 128), F32)], name="norm",
    )
    slots_in = swap(outgoing, 16)
    slots_out = call(ffn_kernel, shape((1024, 256), BF16), slots_in, *weights, name="ffn", flops=10**9)
    results = swap(slots_out, 16)
    gates, take = call(
        gate_kernel, [shape((512, 128), F32), shape((512, 1024), BF16)], slots_out, normed,
        gate_weight.transpose(0, 2, 1).reshape(192, 256), route_row,
        gate_index.reshape(512, 3).T, gate_table, slot, far=(0,), smem=(5,), name="gate",
        flops=2 * 10**9,
    )
    out = call(final_kernel, shape((3, 512, 256), BF16), results, take, gates, name="final")
    return out.reshape(TASKS, 1, 512, 1, 256)


def solution(mesh):
    in_specs = (
        P("batch", "seq", None, None),
        P(None, None, "seq"),
        P(),
        P("seq", "batch", None),
        P("seq", "batch", None),
        P(),
        P(),
        P("batch", "seq", None, None),
        P("batch", "seq", None, None),
    )
    out_specs = P(None, "batch", "seq", None, None)
    return jax.shard_map(
        on_device, mesh=mesh, in_specs=in_specs, out_specs=out_specs, check_vma=False
    )
```

```python
import functools

import jax
import jax.numpy as jnp
import ml_dtypes
import numpy as np
from jax import lax
from jax.experimental import pallas as pl
from jax.experimental.pallas import tpu as pltpu
from jax.sharding import PartitionSpec as P

EXPERTS = 64
TASKS = 3
CAP = 16
ROWS = 256
COLS = 128
LENGTH = ROWS * COLS
BF16 = jnp.bfloat16
F32 = jnp.float32

NN = (((1,), (0,)), ((), ()))
NT = (((1,), (1,)), ((), ()))


def dot(a, b, dims):
    return lax.dot_general(a, b, dims, preferred_element_type=F32)


def split(x):
    hi = x.astype(BF16)
    return hi, (x - hi.astype(F32)).astype(BF16)


def np_split(x):
    hi = x.astype(ml_dtypes.bfloat16)
    return hi, (x - hi.astype(np.float64)).astype(ml_dtypes.bfloat16)


def cos_sin(rows, cols, points):
    angle = 2.0 * np.pi * (np.outer(np.arange(rows), np.arange(cols)) % points) / points
    return np.cos(angle), np.sin(angle)


def tables():
    order = np.arange(ROWS).reshape(64, 4).T.reshape(-1)
    cos_r, sin_r = cos_sin(ROWS, ROWS, ROWS)
    cos_c, sin_c = cos_sin(COLS, COLS, COLS)
    tw_cos, tw_sin = cos_sin(ROWS, COLS, LENGTH)
    first = np.concatenate([cos_r[:, order], -sin_r[:, order]], 0)
    second = np.block([[cos_c, sin_c], [-sin_c, cos_c]])
    fourth = np.concatenate([cos_r[order], -sin_r[order]], 0)
    factors = np.concatenate([part for m in (first, second, fourth) for part in np_split(m)])
    turns = [t[i : i + 128] for t in (tw_cos, tw_sin) for i in (0, 128)]
    lane = np.arange(512)
    source = (lane // 16 % 8) * 64 + (lane // 128) * 16 + lane % 16
    lanes = (lane[:, None] == source[None, :]).astype(ml_dtypes.bfloat16)
    return factors, np.stack(turns).astype(np.float32), lanes


def prep_kernel(ev_ref, routes_ref, out_ref, slot_ref, landed, named, mid, wide, sems):
    copies = [
        pltpu.make_async_copy(
            ev_ref.at[pl.ds(pb * 128, 128)], landed.at[pl.ds(pb * 128, 128)], sems.at[pb]
        )
        for pb in range(4)
    ]
    copies.append(pltpu.make_async_copy(routes_ref, named, sems.at[4]))
    for copy in copies[::-1]:
        copy.start()
    copies[4].wait()
    experts = named[...]
    onehot = (lax.broadcasted_iota(jnp.int32, (EXPERTS, 512), 0) == experts).astype(F32)
    before = lax.broadcasted_iota(jnp.int32, (512, 512), 0) < lax.broadcasted_iota(
        jnp.int32, (512, 512), 1
    )
    earlier = dot(onehot.astype(BF16), before.astype(F32).astype(BF16), NN)
    rank = jnp.sum(earlier * onehot, 0, keepdims=True)
    experts = experts.astype(F32)
    slot_ref[...] = jnp.broadcast_to(experts * CAP + rank, (8, 512))
    for pb in range(4):
        for i, row in enumerate((experts, rank)):
            wide[pl.ds(16 + i * 4 + pb, 64, stride=24), :] = jnp.broadcast_to(
                row[:, pb * 128 : (pb + 1) * 128], (64, 128)
            )
    for pb in range(4):
        copies[pb].wait()
        mid[...] = landed[pb * 128 : (pb + 1) * 128, :].astype(F32).T
        for ch in range(4):
            chp, chl = ch // 2, ch % 2
            wide[pl.ds(chl * 8 + pb * 2 + chp, 64, stride=24), :] = mid[pl.ds(ch, 64, stride=4), :]
    out_ref[...] = wide[...].astype(BF16)


def filter_kernel(x_ref, spec_ref, factor_ref, turn_ref, out_ref, wide, sums, stage):
    first = factor_ref[0:512], factor_ref[512:1024]
    second = factor_ref[1024:1280], factor_ref[1280:1536]
    fourth = [
        jnp.concatenate([factor_ref[at : at + 256], factor_ref[at + 256 : at + 512]], 1)
        for at in (1536, 2048)
    ]
    wide[...] = x_ref[...].astype(F32)
    sig = jnp.concatenate(
        [
            jnp.concatenate(
                [
                    wide[pl.ds(ch % 2 * 8 + pb * 2 + ch // 2, 64, stride=24), :]
                    for ch in range(4)
                ],
                1,
            )
            for pb in range(4)
        ],
        0,
    )
    sig16 = sig.astype(BF16)
    spec1 = dot(first[0], sig16, NN) + dot(first[1], sig16, NN)
    tcos, tsin = [jnp.concatenate([turn_ref[i], turn_ref[i + 1]], 0) for i in (0, 2)]
    turned = []
    for ch in range(4):
        re = spec1[:256, ch * 128 : (ch + 1) * 128]
        im = spec1[256:, ch * 128 : (ch + 1) * 128]
        turned.append(jnp.concatenate([re * tcos + im * tsin, im * tcos - re * tsin], 1))
    t_hi, t_lo = split(jnp.concatenate(turned, 0))
    spec2 = (
        dot(second[0], t_hi, NT) + dot(second[0], t_lo, NT) + dot(second[1], t_hi, NT)
    )
    prods = []
    for ch in range(4):
        fr = spec_ref[0, :, ch * 256 : (ch + 1) * 256]
        fi = spec_ref[1, :, ch * 256 : (ch + 1) * 256]
        zr = spec2[:128, ch * 256 : (ch + 1) * 256]
        zi = spec2[128:, ch * 256 : (ch + 1) * 256]
        prods.append(jnp.concatenate([zr * fi + zi * fr, zr * fr - zi * fi], 0))
    p_hi, p_lo = split(jnp.concatenate(prods, 1))
    back = dot(second[0], p_hi, NN) + dot(second[0], p_lo, NN) + dot(second[1], p_hi, NN)
    bcos, bsin = [jnp.concatenate([turn_ref[i].T, turn_ref[i + 1].T], 1) for i in (0, 2)]
    turned = []
    for ch in range(4):
        im = back[:128, ch * 256 : (ch + 1) * 256]
        re = back[128:, ch * 256 : (ch + 1) * 256]
        turned.append(jnp.concatenate([re * bcos - im * bsin, im * bcos + re * bsin], 1))
    v_hi, v_lo = split(jnp.concatenate(turned, 0))
    filtered = (
        dot(fourth[0], v_hi, NT) + dot(fourth[0], v_lo, NT) + dot(fourth[1], v_hi, NT)
    )
    summed = sig + filtered * (1.0 / LENGTH)
    for ch in range(4):
        sums[ch] = summed[:, ch * 128 : (ch + 1) * 128]
    low = lax.broadcasted_iota(jnp.int32, (8, 512), 0).astype(F32)

    def spread(ref_rows):
        return jnp.concatenate([jnp.broadcast_to(r, (8, 128)) for r in ref_rows], 1)

    def place(block):
        at = block * 24 + 16
        expert = spread([wide[pl.ds(at + pb, 1), :] for pb in range(4)])
        rank = spread([wide[pl.ds(at + 4 + pb, 1), :] for pb in range(4)])
        to = jnp.concatenate(
            [jnp.where(expert == low + 8.0 * m, 1.0, 0.0) for m in range(8)], 0
        ).astype(BF16)
        here = [rank == low, rank == low + 8.0]
        values = []
        for ch in range(4):
            vals = spread([sums[ch, pl.ds(pb * 64 + block, 1), :] for pb in range(4)])
            values += [jnp.where(m, vals, 0.0) for m in here]
        return dot(to, jnp.concatenate(values, 0).astype(BF16), NT)

    def group(hi, carry):
        for q in range(4):
            pair = [place(hi * 8 + q * 2 + half) for half in range(2)]
            stage[q, pl.ds(hi, 64, stride=8), :] = jnp.concatenate(pair, 1)
        return carry

    lax.fori_loop(0, 8, group, 0)
    for q in range(4):
        out_ref[:, q * 128 : (q + 1) * 128] = stage[q].astype(BF16)


def ready_kernel(
    after_ref, spec_ref, factor_ref, turn_ref, spec_out, factor_out, turn_out, raw, sems
):
    copies = [
        pltpu.make_async_copy(src, dst, sems.at[i])
        for i, (src, dst) in enumerate(
            ((spec_ref, raw), (factor_ref, factor_out), (turn_ref, turn_out))
        )
    ]
    for copy in copies:
        copy.start()
    copies[0].wait()
    for part in range(2):
        for ch in range(4):
            for half in range(2):
                at = ch * 256 + half * 128
                spec_out[part, :, at : at + 128] = raw[part, pl.ds(4 * half + ch, 128, stride=8), :]
    copies[1].wait()
    copies[2].wait()


def expert_kernel(
    x_ref, lanes_ref, gain_ref, gate_ref, own_ref, one_ref, two_ref, three_ref,
    out_ref, turned, slots, full,
):
    moved = dot(x_ref[...], lanes_ref[...], NN)
    for ch in range(4):
        turned[ch] = moved[:, ch * 128 : (ch + 1) * 128]
    normed = []
    for hi in range(8):
        for ch in range(4):
            slots[pl.ds(ch, 64, stride=4), :] = turned[ch, pl.ds(hi, 64, stride=8), :]
        vals = slots[...]
        centre = jnp.sum(vals, 0, keepdims=True) * (1.0 / 256)
        off = vals - centre
        spread = jnp.sum(off * off, 0, keepdims=True) * (1.0 / 256)
        normed.append((off * lax.rsqrt(spread + 1e-05) * gain_ref[...]).T.astype(BF16))
    normed = jnp.concatenate(normed, 0)
    total = None
    for part in (own_ref, one_ref, two_ref, three_ref):
        hidden = jnp.maximum(dot(normed, part[0], NT), 0.0).astype(BF16)
        term = dot(hidden, part[1], NN)
        total = term if total is None else total + term
    full[:, 0:16, :] = total[:, :128].reshape(64, 16, 128)
    full[:, 16:32, :] = total[:, 128:].reshape(64, 16, 128)
    scores = dot(normed, gate_ref[...], NT).reshape(64, 2, 8, 256)
    full[:, 32:40, :] = scores[:, 0, :, :128] + scores[:, 1, :, 128:]
    out_ref[...] = full[...].astype(BF16)


def take_kernel(after_ref, index_ref, table_ref, slot_ref, take_ref, bias_ref):
    slot = slot_ref[0:1, :]
    slot_col = jnp.broadcast_to(slot, (128, 512)).T[:, 0:1].astype(jnp.int32)
    take_ref[...] = (
        lax.broadcasted_iota(jnp.int32, (512, EXPERTS * CAP), 1) == slot_col
    ).astype(F32).astype(BF16)
    rows = []
    for t in range(TASKS):
        idx = index_ref[t : t + 1, :]
        bias = jnp.zeros((1, 512), F32)
        for r in range(table_ref.shape[1]):
            bias = jnp.where(idx == r, table_ref[t, r], bias)
        rows.append(bias)
    rank = slot - CAP * jnp.floor(slot * (1.0 / CAP))
    rows.append(jnp.where(rank >= CAP // 2, 1.0, 0.0))
    rows.append(jnp.zeros((128 - TASKS - 1, 512), F32))
    bias_ref[...] = jnp.concatenate(rows, 0).T


def final_kernel(slots_ref, take_ref, bias_ref, out_ref):
    low = slots_ref[:, 0:16, :].reshape(1024, 128)
    high = slots_ref[:, 16:32, :].reshape(1024, 128)
    score = slots_ref[...].astype(F32)[:, 32:40, :]
    score = jnp.concatenate([score, score], 1).reshape(1024, 128).astype(BF16)
    rows = dot(take_ref[...], jnp.concatenate([low, high, score], 1), NN)
    bias = bias_ref[...]
    both = rows[:, 256:384]
    chosen = jnp.where(
        bias[:, 3:4] > 0.5, jnp.concatenate([both[:, 64:], both[:, :64]], 1), both
    )
    gates = jax.nn.sigmoid(chosen + bias)
    for t in range(TASKS):
        out_ref[t] = (gates[:, t : t + 1] * rows[:, :256]).astype(BF16)


def call(kernel, outs, *args, scratch=(), smem=(), far=(), flops=0, vmem=32, name=None):
    specs = [
        pl.BlockSpec(memory_space=pltpu.SMEM if i in smem else pl.ANY if i in far else pltpu.VMEM)
        for i in range(len(args))
    ]
    many = isinstance(outs, (tuple, list))
    return pl.pallas_call(
        kernel,
        out_shape=outs,
        in_specs=specs,
        out_specs=[pl.BlockSpec(memory_space=pltpu.VMEM)] * len(outs)
        if many
        else pl.BlockSpec(memory_space=pltpu.VMEM),
        scratch_shapes=list(scratch),
        compiler_params=pltpu.CompilerParams(vmem_limit_bytes=vmem * 2**20),
        cost_estimate=pl.CostEstimate(flops=flops, bytes_accessed=2**20, transcendentals=0),
        name=name,
    )(*args)


def shape(dims, dtype):
    return jax.ShapeDtypeStruct(dims, dtype)


def swap(values, rows):
    lanes = values.shape[-1]
    chunks = values.reshape(64, rows, lanes)
    return lax.all_to_all(chunks, "seq", split_axis=0, concat_axis=0, tiled=True).reshape(
        64 * rows, lanes
    )


def on_device(
    events, spectral_filter, ln_gain, w_in, w_out, gate_weight, gate_table, routes, gate_index
):
    big = pltpu.VMEM
    chunks, slot = call(
        prep_kernel, [shape((1536, 128), BF16), shape((8, 512), F32)],
        events.reshape(512, 256), routes.reshape(1, 512), far=(0, 1), name="prep", vmem=60,
        scratch=[
            big((512, 256), BF16), big((1, 512), jnp.int32), big((256, 128), F32),
            big((1536, 128), F32), pltpu.SemaphoreType.DMA((5,)),
        ],
    )
    arrived = swap(chunks, 24)
    own = jnp.stack([w_in[0], w_out[0]])
    weights = [own] + [
        lax.ppermute(own, "batch", [(i, (i + d) % 4) for i in range(4)]) for d in (1, 3, 2)
    ]
    spec = spectral_filter.reshape(2, 256, 128, 4).transpose(0, 1, 3, 2).reshape(2, 1024, 128)
    factors, turns, lanes = [jnp.asarray(t) for t in tables()]
    spec, factors, turns = call(
        ready_kernel,
        [shape((2, 128, 1024), F32), shape(factors.shape, BF16), shape(turns.shape, F32)],
        chunks, spec, factors, turns, far=(0, 1, 2, 3), name="ready",
        scratch=[big((2, 1024, 128), F32), pltpu.SemaphoreType.DMA((3,))], flops=2 * 10**9,
    )
    sums = call(
        filter_kernel, shape((512, 512), BF16), arrived, spec, factors, turns,
        scratch=[big((1536, 128), F32), big((4, 256, 128), F32), big((4, 512, 128), F32)],
        name="filter", flops=2 * 10**9,
    )
    slots_in = swap(sums, 8)
    me = lax.axis_index("seq")
    gate = lax.dynamic_index_in_dim(gate_weight.transpose(0, 2, 1), me, 1, keepdims=False)
    gate = jnp.zeros((256, 256), BF16).at[0:TASKS].set(gate).at[192 : 192 + TASKS].set(gate)
    slots_out = call(
        expert_kernel, shape((64, 40, 128), BF16),
        slots_in, lanes, ln_gain.reshape(256, 1), gate, *weights, name="expert", flops=10**9,
        scratch=[big((4, 512, 128), F32), big((256, 128), F32), big((64, 40, 128), F32)],
    )
    results = lax.all_to_all(slots_out, "seq", split_axis=0, concat_axis=0, tiled=True)
    take, bias = call(
        take_kernel, [shape((512, 1024), BF16), shape((512, 128), F32)], slots_out,
        gate_index.reshape(512, 3).T, gate_table, slot, far=(0,), smem=(2,), name="take",
        flops=2 * 10**9,
    )
    out = call(final_kernel, shape((3, 512, 256), BF16), results, take, bias, name="final")
    return out.reshape(TASKS, 1, 512, 1, 256)


def solution(mesh):
    in_specs = (
        P("batch", "seq", None, None),
        P(None, None, "seq"),
        P(),
        P("seq", "batch", None),
        P("seq", "batch", None),
        P(),
        P(),
        P("batch", "seq", None, None),
        P("batch", "seq", None, None),
    )
    out_specs = P(None, "batch", "seq", None, None)
    return jax.shard_map(
        on_device, mesh=mesh, in_specs=in_specs, out_specs=out_specs, check_vma=False
    )
```

```python
import functools

import jax
import jax.numpy as jnp
import ml_dtypes
import numpy as np
from jax import lax
from jax.experimental import pallas as pl
from jax.experimental.pallas import tpu as pltpu
from jax.sharding import PartitionSpec as P

EXPERTS = 64
TASKS = 3
CAP = 16
ROWS = 256
COLS = 128
LENGTH = ROWS * COLS
BF16 = jnp.bfloat16
F32 = jnp.float32

NN = (((1,), (0,)), ((), ()))
NT = (((1,), (1,)), ((), ()))


def dot(a, b, dims):
    return lax.dot_general(a, b, dims, preferred_element_type=F32)


def split(x):
    hi = x.astype(BF16)
    return hi, (x - hi.astype(F32)).astype(BF16)


def np_split(x):
    hi = x.astype(ml_dtypes.bfloat16)
    return hi, (x - hi.astype(np.float64)).astype(ml_dtypes.bfloat16)


def cos_sin(rows, cols, points):
    angle = 2.0 * np.pi * (np.outer(np.arange(rows), np.arange(cols)) % points) / points
    return np.cos(angle), np.sin(angle)


def tables():
    order = np.arange(ROWS).reshape(64, 4).T.reshape(-1)
    cos_r, sin_r = cos_sin(ROWS, ROWS, ROWS)
    cos_c, sin_c = cos_sin(COLS, COLS, COLS)
    tw_cos, tw_sin = cos_sin(ROWS, COLS, LENGTH)
    first = np.concatenate([cos_r[:, order], -sin_r[:, order]], 0)
    second = np.block([[cos_c, sin_c], [-sin_c, cos_c]])
    fourth = np.concatenate([cos_r[order], -sin_r[order]], 0)
    factors = np.concatenate([part for m in (first, second, fourth) for part in np_split(m)])
    turns = [t[i : i + 128] for t in (tw_cos, tw_sin) for i in (0, 128)]
    lane = np.arange(512)
    source = (lane // 16 % 8) * 64 + (lane // 128) * 16 + lane % 16
    lanes = (lane[:, None] == source[None, :]).astype(ml_dtypes.bfloat16)
    return factors, np.stack(turns).astype(np.float32), lanes


def prep_kernel(ev_ref, routes_ref, out_ref, slot_ref, landed, named, mid, wide, sems):
    copies = [
        pltpu.make_async_copy(
            ev_ref.at[pl.ds(pb * 128, 128)], landed.at[pl.ds(pb * 128, 128)], sems.at[pb]
        )
        for pb in range(4)
    ]
    copies.append(pltpu.make_async_copy(routes_ref, named, sems.at[4]))
    for copy in copies[::-1]:
        copy.start()
    copies[4].wait()
    experts = named[...]
    onehot = (lax.broadcasted_iota(jnp.int32, (EXPERTS, 512), 0) == experts).astype(F32)
    before = lax.broadcasted_iota(jnp.int32, (512, 512), 0) < lax.broadcasted_iota(
        jnp.int32, (512, 512), 1
    )
    earlier = dot(onehot.astype(BF16), before.astype(F32).astype(BF16), NN)
    rank = jnp.sum(earlier * onehot, 0, keepdims=True)
    experts = experts.astype(F32)
    slot_ref[...] = jnp.broadcast_to(experts * CAP + rank, (8, 512))
    for pb in range(4):
        for i, row in enumerate((experts, rank)):
            wide[pl.ds(16 + i * 4 + pb, 64, stride=24), :] = jnp.broadcast_to(
                row[:, pb * 128 : (pb + 1) * 128], (64, 128)
            )
    for pb in range(4):
        copies[pb].wait()
        mid[...] = landed[pb * 128 : (pb + 1) * 128, :].astype(F32).T
        for ch in range(4):
            chp, chl = ch // 2, ch % 2
            wide[pl.ds(chl * 8 + pb * 2 + chp, 64, stride=24), :] = mid[pl.ds(ch, 64, stride=4), :]
    out_ref[...] = wide[...].astype(BF16)


def filter_kernel(x_ref, spec_ref, factor_ref, turn_ref, out_ref, wide, sums, stage):
    first = factor_ref[0:512], factor_ref[512:1024]
    second = factor_ref[1024:1280], factor_ref[1280:1536]
    fourth = [
        jnp.concatenate([factor_ref[at : at + 256], factor_ref[at + 256 : at + 512]], 1)
        for at in (1536, 2048)
    ]
    wide[...] = x_ref[...].astype(F32)
    sig = jnp.concatenate(
        [
            jnp.concatenate(
                [
                    wide[pl.ds(ch % 2 * 8 + pb * 2 + ch // 2, 64, stride=24), :]
                    for ch in range(4)
                ],
                1,
            )
            for pb in range(4)
        ],
        0,
    )
    sig16 = sig.astype(BF16)
    spec1 = dot(first[0], sig16, NN) + dot(first[1], sig16, NN)
    tcos, tsin = [jnp.concatenate([turn_ref[i], turn_ref[i + 1]], 0) for i in (0, 2)]
    turned = []
    for ch in range(4):
        re = spec1[:256, ch * 128 : (ch + 1) * 128]
        im = spec1[256:, ch * 128 : (ch + 1) * 128]
        turned.append(jnp.concatenate([re * tcos + im * tsin, im * tcos - re * tsin], 1))
    t_hi, t_lo = split(jnp.concatenate(turned, 0))
    spec2 = (
        dot(second[0], t_hi, NT) + dot(second[0], t_lo, NT) + dot(second[1], t_hi, NT)
    )
    prods = []
    for ch in range(4):
        fr = spec_ref[0, :, ch * 256 : (ch + 1) * 256]
        fi = spec_ref[1, :, ch * 256 : (ch + 1) * 256]
        zr = spec2[:128, ch * 256 : (ch + 1) * 256]
        zi = spec2[128:, ch * 256 : (ch + 1) * 256]
        prods.append(jnp.concatenate([zr * fi + zi * fr, zr * fr - zi * fi], 0))
    p_hi, p_lo = split(jnp.concatenate(prods, 1))
    back = dot(second[0], p_hi, NN) + dot(second[0], p_lo, NN) + dot(second[1], p_hi, NN)
    bcos, bsin = [jnp.concatenate([turn_ref[i].T, turn_ref[i + 1].T], 1) for i in (0, 2)]
    turned = []
    for ch in range(4):
        im = back[:128, ch * 256 : (ch + 1) * 256]
        re = back[128:, ch * 256 : (ch + 1) * 256]
        turned.append(jnp.concatenate([re * bcos - im * bsin, im * bcos + re * bsin], 1))
    v_hi, v_lo = split(jnp.concatenate(turned, 0))
    filtered = (
        dot(fourth[0], v_hi, NT) + dot(fourth[0], v_lo, NT) + dot(fourth[1], v_hi, NT)
    )
    summed = sig + filtered * (1.0 / LENGTH)
    for ch in range(4):
        sums[ch] = summed[:, ch * 128 : (ch + 1) * 128]
    low = lax.broadcasted_iota(jnp.int32, (8, 512), 0).astype(F32)

    def spread(ref_rows):
        return jnp.concatenate([jnp.broadcast_to(r, (8, 128)) for r in ref_rows], 1)

    def place(block):
        at = block * 24 + 16
        expert = spread([wide[pl.ds(at + pb, 1), :] for pb in range(4)])
        rank = spread([wide[pl.ds(at + 4 + pb, 1), :] for pb in range(4)])
        to = jnp.concatenate(
            [jnp.where(expert == low + 8.0 * m, 1.0, 0.0) for m in range(8)], 0
        ).astype(BF16)
        here = [rank == low, rank == low + 8.0]
        values = []
        for ch in range(4):
            vals = spread([sums[ch, pl.ds(pb * 64 + block, 1), :] for pb in range(4)])
            values += [jnp.where(m, vals, 0.0) for m in here]
        return dot(to, jnp.concatenate(values, 0).astype(BF16), NT)

    def group(hi, carry):
        for q in range(4):
            pair = [place(hi * 8 + q * 2 + half) for half in range(2)]
            stage[q, pl.ds(hi, 64, stride=8), :] = jnp.concatenate(pair, 1)
        return carry

    lax.fori_loop(0, 8, group, 0, unroll=8)
    for q in range(4):
        out_ref[:, q * 128 : (q + 1) * 128] = stage[q].astype(BF16)


def ready_kernel(
    after_ref, spec_ref, factor_ref, turn_ref, spec_out, factor_out, turn_out, raw, sems
):
    copies = [
        pltpu.make_async_copy(src, dst, sems.at[i])
        for i, (src, dst) in enumerate(
            ((spec_ref, raw), (factor_ref, factor_out), (turn_ref, turn_out))
        )
    ]
    for copy in copies:
        copy.start()
    copies[0].wait()
    for part in range(2):
        for ch in range(4):
            for half in range(2):
                at = ch * 256 + half * 128
                spec_out[part, :, at : at + 128] = raw[part, pl.ds(4 * half + ch, 128, stride=8), :]
    copies[1].wait()
    copies[2].wait()


def expert_kernel(
    x_ref, lanes_ref, gain_ref, gate_ref, *refs
):
    out_ref, turned, slots, full = refs[8:]
    moved = dot(x_ref[...], lanes_ref[...], NN)
    for ch in range(4):
        turned[ch] = moved[:, ch * 128 : (ch + 1) * 128]
    normed = []
    for hi in range(8):
        for ch in range(4):
            slots[pl.ds(ch, 64, stride=4), :] = turned[ch, pl.ds(hi, 64, stride=8), :]
        vals = slots[...]
        centre = jnp.sum(vals, 0, keepdims=True) * (1.0 / 256)
        off = vals - centre
        spread = jnp.sum(off * off, 0, keepdims=True) * (1.0 / 256)
        normed.append((off * lax.rsqrt(spread + 1e-05) * gain_ref[...]).T.astype(BF16))
    normed = jnp.concatenate(normed, 0)
    total = None
    for part_in, part_out in zip(refs[0:8:2], refs[1:8:2]):
        hidden = jnp.maximum(dot(normed, part_in[...], NT), 0.0).astype(BF16)
        term = dot(hidden, part_out[...], NN)
        total = term if total is None else total + term
    full[:, 0:16, :] = total[:, :128].reshape(64, 16, 128)
    full[:, 16:32, :] = total[:, 128:].reshape(64, 16, 128)
    scores = dot(normed, gate_ref[...], NT).reshape(64, 2, 8, 256)
    full[:, 32:40, :] = scores[:, 0, :, :128] + scores[:, 1, :, 128:]
    out_ref[...] = full[...].astype(BF16)


def take_kernel(after_ref, index_ref, table_ref, slot_ref, take_ref, bias_ref):
    slot = slot_ref[0:1, :]
    slot_col = jnp.broadcast_to(slot, (128, 512)).T[:, 0:1].astype(jnp.int32)
    take_ref[...] = (
        lax.broadcasted_iota(jnp.int32, (512, EXPERTS * CAP), 1) == slot_col
    ).astype(F32).astype(BF16)
    rows = []
    for t in range(TASKS):
        idx = index_ref[t : t + 1, :]
        bias = jnp.zeros((1, 512), F32)
        for r in range(table_ref.shape[1]):
            bias = jnp.where(idx == r, table_ref[t, r], bias)
        rows.append(bias)
    rank = slot - CAP * jnp.floor(slot * (1.0 / CAP))
    rows.append(jnp.where(rank >= CAP // 2, 1.0, 0.0))
    rows.append(jnp.zeros((128 - TASKS - 1, 512), F32))
    bias_ref[...] = jnp.concatenate(rows, 0).T


def final_kernel(slots_ref, take_ref, bias_ref, out_ref):
    low = slots_ref[:, 0:16, :].reshape(1024, 128)
    high = slots_ref[:, 16:32, :].reshape(1024, 128)
    score = slots_ref[...].astype(F32)[:, 32:40, :]
    score = jnp.concatenate([score, score], 1).reshape(1024, 128).astype(BF16)
    rows = dot(take_ref[...], jnp.concatenate([low, high, score], 1), NN)
    bias = bias_ref[...]
    both = rows[:, 256:384]
    chosen = jnp.where(
        bias[:, 3:4] > 0.5, jnp.concatenate([both[:, 64:], both[:, :64]], 1), both
    )
    gates = jax.nn.sigmoid(chosen + bias)
    for t in range(TASKS):
        out_ref[t] = (gates[:, t : t + 1] * rows[:, :256]).astype(BF16)


def call(kernel, outs, *args, scratch=(), smem=(), far=(), flops=0, vmem=32, name=None):
    specs = [
        pl.BlockSpec(memory_space=pltpu.SMEM if i in smem else pl.ANY if i in far else pltpu.VMEM)
        for i in range(len(args))
    ]
    many = isinstance(outs, (tuple, list))
    return pl.pallas_call(
        kernel,
        out_shape=outs,
        in_specs=specs,
        out_specs=[pl.BlockSpec(memory_space=pltpu.VMEM)] * len(outs)
        if many
        else pl.BlockSpec(memory_space=pltpu.VMEM),
        scratch_shapes=list(scratch),
        compiler_params=pltpu.CompilerParams(vmem_limit_bytes=vmem * 2**20),
        cost_estimate=pl.CostEstimate(flops=flops, bytes_accessed=2**20, transcendentals=0),
        name=name,
    )(*args)


def shape(dims, dtype):
    return jax.ShapeDtypeStruct(dims, dtype)


def swap(values, rows):
    lanes = values.shape[-1]
    chunks = values.reshape(64, rows, lanes)
    return lax.all_to_all(chunks, "seq", split_axis=0, concat_axis=0, tiled=True).reshape(
        64 * rows, lanes
    )


def on_device(
    events, spectral_filter, ln_gain, w_in, w_out, gate_weight, gate_table, routes, gate_index
):
    big = pltpu.VMEM
    chunks, slot = call(
        prep_kernel, [shape((1536, 128), BF16), shape((8, 512), F32)],
        events.reshape(512, 256), routes.reshape(1, 512), far=(0, 1), name="prep", vmem=60,
        scratch=[
            big((512, 256), BF16), big((1, 512), jnp.int32), big((256, 128), F32),
            big((1536, 128), F32), pltpu.SemaphoreType.DMA((5,)),
        ],
    )
    arrived = swap(chunks, 24)
    ahead, behind = [(i, (i + 1) % 4) for i in range(4)], [(i, (i + 3) % 4) for i in range(4)]
    own_in, own_out = w_in[0], w_out[0]
    one_in = lax.ppermute(own_in, "batch", ahead)
    two_out = lax.ppermute(own_out, "batch", behind)
    far_in = lax.ppermute(one_in, "batch", ahead)
    far_out = lax.ppermute(two_out, "batch", behind)
    one_out = lax.ppermute(own_out, "batch", ahead)
    two_in = lax.ppermute(own_in, "batch", behind)
    spec = spectral_filter.reshape(2, 256, 128, 4).transpose(0, 1, 3, 2).reshape(2, 1024, 128)
    factors, turns, lanes = [jnp.asarray(t) for t in tables()]
    spec, factors, turns = call(
        ready_kernel,
        [shape((2, 128, 1024), F32), shape(factors.shape, BF16), shape(turns.shape, F32)],
        chunks, spec, factors, turns, far=(0, 1, 2, 3), name="ready",
        scratch=[big((2, 1024, 128), F32), pltpu.SemaphoreType.DMA((3,))], flops=2 * 10**9,
    )
    sums = call(
        filter_kernel, shape((512, 512), BF16), arrived, spec, factors, turns,
        scratch=[big((1536, 128), F32), big((4, 256, 128), F32), big((4, 512, 128), F32)],
        name="filter", flops=2 * 10**9,
    )
    slots_in = swap(sums, 8)
    me = lax.axis_index("seq")
    gate = lax.dynamic_index_in_dim(gate_weight.transpose(0, 2, 1), me, 1, keepdims=False)
    gate = jnp.zeros((256, 256), BF16).at[0:TASKS].set(gate).at[192 : 192 + TASKS].set(gate)
    slots_out = call(
        expert_kernel, shape((64, 40, 128), BF16),
        slots_in, lanes, ln_gain.reshape(256, 1), gate,
        own_in, own_out, one_in, one_out, two_in, two_out, far_in, far_out,
        name="expert", flops=10**9,
        scratch=[big((4, 512, 128), F32), big((256, 128), F32), big((64, 40, 128), F32)],
    )
    results = lax.all_to_all(slots_out, "seq", split_axis=0, concat_axis=0, tiled=True)
    take, bias = call(
        take_kernel, [shape((512, 1024), BF16), shape((512, 128), F32)], slots_out,
        gate_index.reshape(512, 3).T, gate_table, slot, far=(0,), smem=(2,), name="take",
        flops=2 * 10**9,
    )
    out = call(final_kernel, shape((3, 512, 256), BF16), results, take, bias, name="final")
    return out.reshape(TASKS, 1, 512, 1, 256)


def solution(mesh):
    in_specs = (
        P("batch", "seq", None, None),
        P(None, None, "seq"),
        P(),
        P("seq", "batch", None),
        P("seq", "batch", None),
        P(),
        P(),
        P("batch", "seq", None, None),
        P("batch", "seq", None, None),
    )
    out_specs = P(None, "batch", "seq", None, None)
    return jax.shard_map(
        on_device, mesh=mesh, in_specs=in_specs, out_specs=out_specs, check_vma=False
    )
```

```python
import functools

import jax
import jax.numpy as jnp
import ml_dtypes
import numpy as np
from jax import lax
from jax.experimental import pallas as pl
from jax.experimental.pallas import tpu as pltpu
from jax.sharding import PartitionSpec as P

EXPERTS = 64
TASKS = 3
CAP = 16
ROWS = 256
COLS = 128
LENGTH = ROWS * COLS
BF16 = jnp.bfloat16
F32 = jnp.float32

NN = (((1,), (0,)), ((), ()))
NT = (((1,), (1,)), ((), ()))


def dot(a, b, dims):
    return lax.dot_general(a, b, dims, preferred_element_type=F32)


def split(x):
    hi = x.astype(BF16)
    return hi, (x - hi.astype(F32)).astype(BF16)


def np_split(x):
    hi = x.astype(ml_dtypes.bfloat16)
    return hi, (x - hi.astype(np.float64)).astype(ml_dtypes.bfloat16)


def cos_sin(rows, cols, points):
    angle = 2.0 * np.pi * (np.outer(np.arange(rows), np.arange(cols)) % points) / points
    return np.cos(angle), np.sin(angle)


def tables():
    cos_r, sin_r = cos_sin(ROWS, ROWS, ROWS)
    cos_c, sin_c = cos_sin(COLS, COLS, COLS)
    tw_cos, tw_sin = cos_sin(ROWS, COLS, LENGTH)
    first = np.concatenate([cos_r, -sin_r], 0)
    second = np.block([[cos_c, sin_c], [-sin_c, cos_c]])
    factors = np.concatenate([part for m in (first, second) for part in np_split(m)])
    turns = [t[i : i + 128] for t in (tw_cos, tw_sin) for i in (0, 128)]
    lane = np.arange(512)
    source = (lane // 16 % 8) * 64 + (lane // 128) * 16 + lane % 16
    lanes = (lane[:, None] == source[None, :]).astype(ml_dtypes.bfloat16)
    return factors, np.stack(turns).astype(np.float32), lanes


def prep_kernel(ev_ref, routes_ref, out_ref, slot_ref, landed, named, mid, wide, sems):
    copies = [
        pltpu.make_async_copy(
            ev_ref.at[pl.ds(pb * 128, 128)], landed.at[pl.ds(pb * 128, 128)], sems.at[pb]
        )
        for pb in range(4)
    ]
    copies.append(pltpu.make_async_copy(routes_ref, named, sems.at[4]))
    for copy in copies[::-1]:
        copy.start()
    copies[4].wait()
    experts = named[...]
    onehot = (lax.broadcasted_iota(jnp.int32, (EXPERTS, 512), 0) == experts).astype(F32)
    before = lax.broadcasted_iota(jnp.int32, (512, 512), 0) < lax.broadcasted_iota(
        jnp.int32, (512, 512), 1
    )
    earlier = dot(onehot.astype(BF16), before.astype(F32).astype(BF16), NN)
    rank = jnp.sum(earlier * onehot, 0, keepdims=True)
    experts = experts.astype(F32)
    slot_ref[...] = jnp.broadcast_to(experts * CAP + rank, (8, 512))
    for pb in range(4):
        for i, row in enumerate((experts, rank)):
            wide[pl.ds(16 + i * 4 + pb, 64, stride=24), :] = jnp.broadcast_to(
                row[:, pb * 128 : (pb + 1) * 128], (64, 128)
            )
    for pb in range(4):
        copies[pb].wait()
        mid[...] = landed[pb * 128 : (pb + 1) * 128, :].astype(F32).T
        for ch in range(4):
            chp, chl = ch // 2, ch % 2
            wide[pl.ds(chl * 8 + pb * 2 + chp, 64, stride=24), :] = mid[pl.ds(ch, 64, stride=4), :]
    out_ref[...] = wide[...].astype(BF16)


def filter_kernel(x_ref, spec_ref, factor_ref, turn_ref, out_ref, wide, sums, stage):
    first = factor_ref[0:512], factor_ref[512:1024]
    second = factor_ref[1024:1280], factor_ref[1280:1536]
    fourth = [jnp.concatenate([part[:256], part[256:]], 1) for part in first]
    wide[...] = x_ref[...].astype(F32)
    for ch in range(4):
        for pb in range(4):
            sums[ch, pl.ds(pb, 64, stride=4), :] = wide[
                pl.ds(ch % 2 * 8 + pb * 2 + ch // 2, 64, stride=24), :
            ]
    sig = jnp.concatenate([sums[ch] for ch in range(4)], 1)
    sig16 = sig.astype(BF16)
    spec1 = dot(first[0], sig16, NN) + dot(first[1], sig16, NN)
    tcos, tsin = [jnp.concatenate([turn_ref[i], turn_ref[i + 1]], 0) for i in (0, 2)]
    turned = []
    for ch in range(4):
        re = spec1[:256, ch * 128 : (ch + 1) * 128]
        im = spec1[256:, ch * 128 : (ch + 1) * 128]
        turned.append(jnp.concatenate([re * tcos + im * tsin, im * tcos - re * tsin], 1))
    t_hi, t_lo = split(jnp.concatenate(turned, 0))
    spec2 = (
        dot(second[0], t_hi, NT) + dot(second[0], t_lo, NT) + dot(second[1], t_hi, NT)
    )
    prods = []
    for ch in range(4):
        fr = spec_ref[0, :, ch * 256 : (ch + 1) * 256]
        fi = spec_ref[1, :, ch * 256 : (ch + 1) * 256]
        zr = spec2[:128, ch * 256 : (ch + 1) * 256]
        zi = spec2[128:, ch * 256 : (ch + 1) * 256]
        prods.append(jnp.concatenate([zr * fi + zi * fr, zr * fr - zi * fi], 0))
    p_hi, p_lo = split(jnp.concatenate(prods, 1))
    back = dot(second[0], p_hi, NN) + dot(second[0], p_lo, NN) + dot(second[1], p_hi, NN)
    bcos, bsin = [jnp.concatenate([turn_ref[i].T, turn_ref[i + 1].T], 1) for i in (0, 2)]
    turned = []
    for ch in range(4):
        im = back[:128, ch * 256 : (ch + 1) * 256]
        re = back[128:, ch * 256 : (ch + 1) * 256]
        turned.append(jnp.concatenate([re * bcos - im * bsin, im * bcos + re * bsin], 1))
    v_hi, v_lo = split(jnp.concatenate(turned, 0))
    filtered = (
        dot(fourth[0], v_hi, NT) + dot(fourth[0], v_lo, NT) + dot(fourth[1], v_hi, NT)
    )
    summed = sig + filtered * (1.0 / LENGTH)
    for ch in range(4):
        sums[ch] = summed[:, ch * 128 : (ch + 1) * 128]
    low = lax.broadcasted_iota(jnp.int32, (8, 512), 0).astype(F32)

    def spread(ref_rows):
        return jnp.concatenate([jnp.broadcast_to(r, (8, 128)) for r in ref_rows], 1)

    def place(block):
        at = block * 24 + 16
        expert = spread([wide[pl.ds(at + pb, 1), :] for pb in range(4)])
        rank = spread([wide[pl.ds(at + 4 + pb, 1), :] for pb in range(4)])
        to = jnp.concatenate(
            [jnp.where(expert == low + 8.0 * m, 1.0, 0.0) for m in range(8)], 0
        ).astype(BF16)
        here = [rank == low, rank == low + 8.0]
        values = []
        for ch in range(4):
            vals = spread([sums[ch, pl.ds(block * 4 + pb, 1), :] for pb in range(4)])
            values += [jnp.where(m, vals, 0.0) for m in here]
        return dot(to, jnp.concatenate(values, 0).astype(BF16), NT)

    def group(hi, carry):
        for q in range(4):
            pair = [place(hi * 8 + q * 2 + half) for half in range(2)]
            stage[q, pl.ds(hi, 64, stride=8), :] = jnp.concatenate(pair, 1)
        return carry

    lax.fori_loop(0, 8, group, 0, unroll=8)
    for q in range(4):
        out_ref[:, q * 128 : (q + 1) * 128] = stage[q].astype(BF16)


def ready_kernel(
    after_ref, spec_ref, factor_ref, turn_ref, spec_out, factor_out, turn_out, raw, sems
):
    copies = [
        pltpu.make_async_copy(src, dst, sems.at[i])
        for i, (src, dst) in enumerate(
            ((spec_ref, raw), (factor_ref, factor_out), (turn_ref, turn_out))
        )
    ]
    for copy in copies:
        copy.start()
    copies[0].wait()
    for part in range(2):
        for ch in range(4):
            for half in range(2):
                at = ch * 256 + half * 128
                spec_out[part, :, at : at + 128] = raw[part, pl.ds(4 * half + ch, 128, stride=8), :]
    copies[1].wait()
    copies[2].wait()


def expert_kernel(
    x_ref, lanes_ref, gain_ref, gate_ref, *refs
):
    out_ref, turned, slots, full = refs[8:]
    moved = dot(x_ref[...], lanes_ref[...], NN)
    for ch in range(4):
        turned[ch] = moved[:, ch * 128 : (ch + 1) * 128]
    normed = []
    for hi in range(8):
        for ch in range(4):
            slots[pl.ds(ch, 64, stride=4), :] = turned[ch, pl.ds(hi, 64, stride=8), :]
        vals = slots[...]
        centre = jnp.sum(vals, 0, keepdims=True) * (1.0 / 256)
        off = vals - centre
        spread = jnp.sum(off * off, 0, keepdims=True) * (1.0 / 256)
        normed.append((off * lax.rsqrt(spread + 1e-05) * gain_ref[...]).T.astype(BF16))
    normed = jnp.concatenate(normed, 0)
    total = None
    for part_in, part_out in zip(refs[0:8:2], refs[1:8:2]):
        hidden = jnp.maximum(dot(normed, part_in[...], NT), 0.0).astype(BF16)
        term = dot(hidden, part_out[...], NN)
        total = term if total is None else total + term
    for block in range(64):
        rows = total[block * 16 : (block + 1) * 16]
        full[block * 34 : block * 34 + 16, :] = rows[:, :128]
        full[block * 34 + 16 : block * 34 + 32, :] = rows[:, 128:]
    scores = dot(normed, gate_ref[...], NT)
    own_lanes = lax.broadcasted_iota(jnp.int32, (1024, 128), 1) // 16 == (
        lax.broadcasted_iota(jnp.int32, (1024, 128), 0) % 8
    )
    row = lax.broadcasted_iota(jnp.int32, (128, 1024), 0)
    gather = lax.broadcasted_iota(jnp.int32, (128, 1024), 1) // 8 == row % 64 * 2 + row // 64
    packed = dot(
        jnp.where(gather, 1.0, 0.0).astype(BF16), jnp.where(own_lanes, scores, 0.0).astype(BF16), NN
    )
    for half in range(2):
        full[pl.ds(32 + half, 64, stride=34), :] = packed[half * 64 : (half + 1) * 64]
    out_ref[...] = full[...].astype(BF16)


def take_kernel(
    after_ref, index_ref, table_ref, slot_ref, take_ref, score_ref, lanes_ref, bias_ref
):
    slot = slot_ref[0:1, :]
    expert = jnp.floor(slot * (1.0 / CAP))
    rank = slot - CAP * expert
    half = jnp.where(rank >= CAP // 2, 1.0, 0.0)
    codes = [rank * 64 + expert, half * 64 + expert, rank - CAP // 2 * half]
    codes = jnp.concatenate(codes + [jnp.zeros((125, 512), F32)], 0).T.astype(jnp.int32)
    take_ref[...] = (
        lax.broadcasted_iota(jnp.int32, (512, EXPERTS * CAP), 1) == codes[:, 0:1]
    ).astype(F32).astype(BF16)
    lane = lax.broadcasted_iota(jnp.int32, (512, 128), 1)
    score_ref[...] = (lane == codes[:, 1:2]).astype(F32).astype(BF16)
    lanes_ref[...] = (lane // 16 == codes[:, 2:3]).astype(F32)
    rows = []
    for t in range(TASKS):
        idx = index_ref[t : t + 1, :]
        bias = jnp.zeros((1, 512), F32)
        for r in range(table_ref.shape[1]):
            bias = jnp.where(idx == r, table_ref[t, r], bias)
        rows.append(bias)
    rows.append(jnp.zeros((128 - TASKS, 512), F32))
    bias_ref[...] = jnp.concatenate(rows, 0).T


def final_kernel(slots_ref, take_ref, score_ref, lanes_ref, bias_ref, out_ref, wide):
    wide[...] = slots_ref[...].astype(F32)

    def rows_of(at, count):
        return jnp.concatenate(
            [wide[pl.ds(at + r, 64, stride=34), :] for r in range(count)], 0
        ).astype(BF16)

    gates = dot(score_ref[...], rows_of(32, 2), NN) * lanes_ref[...]
    for shift in (64, 32, 16):
        gates = gates + pltpu.roll(gates, shift, 1)
    gates = jax.nn.sigmoid(gates + bias_ref[...])
    rows = dot(take_ref[...], jnp.concatenate([rows_of(0, 16), rows_of(16, 16)], 1), NN)
    for t in range(TASKS):
        out_ref[t] = (gates[:, t : t + 1] * rows).astype(BF16)


def call(kernel, outs, *args, scratch=(), smem=(), far=(), flops=0, vmem=32, name=None):
    specs = [
        pl.BlockSpec(memory_space=pltpu.SMEM if i in smem else pl.ANY if i in far else pltpu.VMEM)
        for i in range(len(args))
    ]
    many = isinstance(outs, (tuple, list))
    return pl.pallas_call(
        kernel,
        out_shape=outs,
        in_specs=specs,
        out_specs=[pl.BlockSpec(memory_space=pltpu.VMEM)] * len(outs)
        if many
        else pl.BlockSpec(memory_space=pltpu.VMEM),
        scratch_shapes=list(scratch),
        compiler_params=pltpu.CompilerParams(vmem_limit_bytes=vmem * 2**20),
        cost_estimate=pl.CostEstimate(flops=flops, bytes_accessed=2**20, transcendentals=0),
        name=name,
    )(*args)


def shape(dims, dtype):
    return jax.ShapeDtypeStruct(dims, dtype)


def swap(values, rows):
    lanes = values.shape[-1]
    chunks = values.reshape(64, rows, lanes)
    return lax.all_to_all(chunks, "seq", split_axis=0, concat_axis=0, tiled=True).reshape(
        64 * rows, lanes
    )


def on_device(
    events, spectral_filter, ln_gain, w_in, w_out, gate_weight, gate_table, routes, gate_index
):
    big = pltpu.VMEM
    chunks, slot = call(
        prep_kernel, [shape((1536, 128), BF16), shape((8, 512), F32)],
        events.reshape(512, 256), routes.reshape(1, 512), far=(0, 1), name="prep", vmem=60,
        scratch=[
            big((512, 256), BF16), big((1, 512), jnp.int32), big((256, 128), F32),
            big((1536, 128), F32), pltpu.SemaphoreType.DMA((5,)),
        ],
    )
    arrived = swap(chunks, 24)
    ahead, behind = [(i, (i + 1) % 4) for i in range(4)], [(i, (i + 3) % 4) for i in range(4)]
    own_in, own_out = w_in[0], w_out[0]
    one_in = lax.ppermute(own_in, "batch", ahead)
    two_out = lax.ppermute(own_out, "batch", behind)
    far_in = lax.ppermute(one_in, "batch", ahead)
    far_out = lax.ppermute(two_out, "batch", behind)
    one_out = lax.ppermute(own_out, "batch", ahead)
    two_in = lax.ppermute(own_in, "batch", behind)
    spec = spectral_filter.reshape(2, 256, 128, 4).transpose(0, 1, 3, 2).reshape(2, 1024, 128)
    factors, turns, lanes = [jnp.asarray(t) for t in tables()]
    spec, factors, turns = call(
        ready_kernel,
        [shape((2, 128, 1024), F32), shape(factors.shape, BF16), shape(turns.shape, F32)],
        chunks, spec, factors, turns, far=(0, 1, 2, 3), name="ready",
        scratch=[big((2, 1024, 128), F32), pltpu.SemaphoreType.DMA((3,))], flops=2 * 10**9,
    )
    sums = call(
        filter_kernel, shape((512, 512), BF16), arrived, spec, factors, turns,
        scratch=[big((1536, 128), F32), big((4, 256, 128), F32), big((4, 512, 128), F32)],
        name="filter", flops=2 * 10**9,
    )
    slots_in = swap(sums, 8)
    me = lax.axis_index("seq")
    gate = lax.dynamic_index_in_dim(gate_weight.transpose(0, 2, 1), me, 1, keepdims=False)
    gate = jnp.tile(jnp.pad(gate, ((0, 16 - TASKS), (0, 0))), (8, 1))
    slots_out = call(
        expert_kernel, shape((64 * 34, 128), BF16),
        slots_in, lanes, ln_gain.reshape(256, 1), gate,
        own_in, own_out, one_in, one_out, two_in, two_out, far_in, far_out,
        name="expert", flops=10**9,
        scratch=[big((4, 512, 128), F32), big((256, 128), F32), big((64 * 34, 128), F32)],
    )
    results = lax.all_to_all(
        slots_out.reshape(64, 17, 2, 128), "seq", split_axis=0, concat_axis=0, tiled=True
    ).reshape(64 * 34, 128)
    take, score, score_lanes, bias = call(
        take_kernel,
        [
            shape((512, 1024), BF16), shape((512, 128), BF16), shape((512, 128), F32),
            shape((512, 128), F32),
        ],
        slots_out, gate_index.reshape(512, 3).T, gate_table, slot, far=(0,), smem=(2,),
        name="take", flops=2 * 10**9,
    )
    out = call(
        final_kernel, shape((3, 512, 256), BF16), results, take, score, score_lanes, bias,
        scratch=[big((64 * 34, 128), F32)], name="final",
    )
    return out.reshape(TASKS, 1, 512, 1, 256)


def solution(mesh):
    in_specs = (
        P("batch", "seq", None, None),
        P(None, None, "seq"),
        P(),
        P("seq", "batch", None),
        P("seq", "batch", None),
        P(),
        P(),
        P("batch", "seq", None, None),
        P("batch", "seq", None, None),
    )
    out_specs = P(None, "batch", "seq", None, None)
    return jax.shard_map(
        on_device, mesh=mesh, in_specs=in_specs, out_specs=out_specs, check_vma=False
    )
```

```python
import functools

import jax
import jax.numpy as jnp
import ml_dtypes
import numpy as np
from jax import lax
from jax.experimental import pallas as pl
from jax.experimental.pallas import tpu as pltpu
from jax.sharding import PartitionSpec as P

EXPERTS = 64
TASKS = 3
CAP = 16
ROWS = 256
COLS = 128
LENGTH = ROWS * COLS
BF16 = jnp.bfloat16
F32 = jnp.float32

NN = (((1,), (0,)), ((), ()))
NT = (((1,), (1,)), ((), ()))


def dot(a, b, dims):
    return lax.dot_general(a, b, dims, preferred_element_type=F32)


def split(x):
    hi = x.astype(BF16)
    return hi, (x - hi.astype(F32)).astype(BF16)


def np_split(x):
    hi = x.astype(ml_dtypes.bfloat16)
    return hi, (x - hi.astype(np.float64)).astype(ml_dtypes.bfloat16)


def cos_sin(rows, cols, points):
    angle = 2.0 * np.pi * (np.outer(np.arange(rows), np.arange(cols)) % points) / points
    return np.cos(angle), np.sin(angle)


def tables():
    cos_r, sin_r = cos_sin(ROWS, ROWS, ROWS)
    cos_c, sin_c = cos_sin(COLS, COLS, COLS)
    tw_cos, tw_sin = cos_sin(ROWS, COLS, LENGTH)
    first = np.concatenate([cos_r, -sin_r], 0)
    second = np.block([[cos_c, sin_c], [-sin_c, cos_c]])
    factors = np.concatenate([part for m in (first, second) for part in np_split(m)])
    turns = [t[i : i + 128] for t in (tw_cos, tw_sin) for i in (0, 128)]
    lane = np.arange(512)
    source = (lane // 16 % 8) * 64 + (lane // 128) * 16 + lane % 16
    lanes = (lane[:, None] == source[None, :]).astype(ml_dtypes.bfloat16)
    return factors, np.stack(turns).astype(np.float32), lanes


def prep_kernel(ev_ref, routes_ref, out_ref, slot_ref, landed, named, before, mid, wide, sems):
    copies = [
        pltpu.make_async_copy(
            ev_ref.at[pl.ds(pb * 128, 128)], landed.at[pl.ds(pb * 128, 128)], sems.at[pb]
        )
        for pb in range(4)
    ]
    copies.append(pltpu.make_async_copy(routes_ref, named, sems.at[4]))
    for copy in copies[::-1]:
        copy.start()
    before[...] = (
        lax.broadcasted_iota(jnp.int32, (512, 512), 0)
        < lax.broadcasted_iota(jnp.int32, (512, 512), 1)
    ).astype(F32).astype(BF16)
    copies[4].wait()
    experts = named[...]
    onehot = (lax.broadcasted_iota(jnp.int32, (EXPERTS, 512), 0) == experts).astype(F32)
    earlier = dot(onehot.astype(BF16), before[...], NN)
    rank = jnp.sum(earlier * onehot, 0, keepdims=True)
    experts = experts.astype(F32)
    slot_ref[...] = jnp.broadcast_to(experts * CAP + rank, (8, 512))
    for pb in range(4):
        for i, row in enumerate((experts, rank)):
            wide[pl.ds(16 + i * 4 + pb, 64, stride=24), :] = jnp.broadcast_to(
                row[:, pb * 128 : (pb + 1) * 128], (64, 128)
            )
    for pb in range(4):
        copies[pb].wait()
        mid[...] = landed[pb * 128 : (pb + 1) * 128, :].T.astype(F32)
        for ch in range(4):
            chp, chl = ch // 2, ch % 2
            wide[pl.ds(chl * 8 + pb * 2 + chp, 64, stride=24), :] = mid[pl.ds(ch, 64, stride=4), :]
    out_ref[...] = wide[...].astype(BF16)


def filter_kernel(x_ref, spec_ref, factor_ref, turn_ref, out_ref, wide, sums, stage):
    first = factor_ref[0:512], factor_ref[512:1024]
    second = factor_ref[1024:1280], factor_ref[1280:1536]
    fourth = [jnp.concatenate([part[:256], part[256:]], 1) for part in first]
    wide[...] = x_ref[...].astype(F32)
    for ch in range(4):
        for pb in range(4):
            sums[ch, pl.ds(pb, 64, stride=4), :] = wide[
                pl.ds(ch % 2 * 8 + pb * 2 + ch // 2, 64, stride=24), :
            ]
    sig = jnp.concatenate([sums[ch] for ch in range(4)], 1)
    sig16 = sig.astype(BF16)
    spec1 = dot(first[0], sig16, NN) + dot(first[1], sig16, NN)
    tcos, tsin = [jnp.concatenate([turn_ref[i], turn_ref[i + 1]], 0) for i in (0, 2)]
    turned = []
    for ch in range(4):
        re = spec1[:256, ch * 128 : (ch + 1) * 128]
        im = spec1[256:, ch * 128 : (ch + 1) * 128]
        turned.append(jnp.concatenate([re * tcos + im * tsin, im * tcos - re * tsin], 1))
    t_hi, t_lo = split(jnp.concatenate(turned, 0))
    spec2 = (
        dot(second[0], t_hi, NT) + dot(second[0], t_lo, NT) + dot(second[1], t_hi, NT)
    )
    prods = []
    for ch in range(4):
        fr = spec_ref[0, :, ch * 256 : (ch + 1) * 256]
        fi = spec_ref[1, :, ch * 256 : (ch + 1) * 256]
        zr = spec2[:128, ch * 256 : (ch + 1) * 256]
        zi = spec2[128:, ch * 256 : (ch + 1) * 256]
        prods.append(jnp.concatenate([zr * fi + zi * fr, zr * fr - zi * fi], 0))
    p_hi, p_lo = split(jnp.concatenate(prods, 1))
    back = dot(second[0], p_hi, NN) + dot(second[0], p_lo, NN) + dot(second[1], p_hi, NN)
    bcos, bsin = [jnp.concatenate([turn_ref[i].T, turn_ref[i + 1].T], 1) for i in (0, 2)]
    turned = []
    for ch in range(4):
        im = back[:128, ch * 256 : (ch + 1) * 256]
        re = back[128:, ch * 256 : (ch + 1) * 256]
        turned.append(jnp.concatenate([re * bcos - im * bsin, im * bcos + re * bsin], 1))
    v_hi, v_lo = split(jnp.concatenate(turned, 0))
    filtered = (
        dot(fourth[0], v_hi, NT) + dot(fourth[0], v_lo, NT) + dot(fourth[1], v_hi, NT)
    )
    summed = sig + filtered * (1.0 / LENGTH)
    for ch in range(4):
        sums[ch] = summed[:, ch * 128 : (ch + 1) * 128]
    low = lax.broadcasted_iota(jnp.int32, (8, 512), 0).astype(F32)

    def spread(ref_rows):
        return jnp.concatenate([jnp.broadcast_to(r, (8, 128)) for r in ref_rows], 1)

    def place(block):
        at = block * 24 + 16
        expert = spread([wide[pl.ds(at + pb, 1), :] for pb in range(4)])
        rank = spread([wide[pl.ds(at + 4 + pb, 1), :] for pb in range(4)])
        to = jnp.concatenate(
            [jnp.where(expert == low + 8.0 * m, 1.0, 0.0) for m in range(8)], 0
        ).astype(BF16)
        here = [rank == low, rank == low + 8.0]
        values = []
        for ch in range(4):
            vals = spread([sums[ch, pl.ds(block * 4 + pb, 1), :] for pb in range(4)])
            values += [jnp.where(m, vals, 0.0) for m in here]
        return dot(to, jnp.concatenate(values, 0).astype(BF16), NT)

    def group(hi, carry):
        for q in range(4):
            pair = [place(hi * 8 + q * 2 + half) for half in range(2)]
            stage[q, pl.ds(hi, 64, stride=8), :] = jnp.concatenate(pair, 1)
        return carry

    lax.fori_loop(0, 8, group, 0, unroll=8)
    for q in range(4):
        out_ref[:, q * 128 : (q + 1) * 128] = stage[q].astype(BF16)


def ready_kernel(
    after_ref, spec_ref, factor_ref, turn_ref, spec_out, factor_out, turn_out, raw, sems
):
    copies = [
        pltpu.make_async_copy(src, dst, sems.at[i])
        for i, (src, dst) in enumerate(
            ((spec_ref, raw), (factor_ref, factor_out), (turn_ref, turn_out))
        )
    ]
    for copy in copies:
        copy.start()
    copies[0].wait()
    for part in range(2):
        for ch in range(4):
            for half in range(2):
                at = ch * 256 + half * 128
                spec_out[part, :, at : at + 128] = raw[part, pl.ds(4 * half + ch, 128, stride=8), :]
    copies[1].wait()
    copies[2].wait()


def expert_kernel(
    x_ref, lanes_ref, gain_ref, gate_ref, *refs
):
    out_ref, turned, slots, full = refs[8:]
    moved = dot(x_ref[...], lanes_ref[...], NN)
    for ch in range(4):
        turned[ch] = moved[:, ch * 128 : (ch + 1) * 128]
    normed = []
    for hi in range(8):
        for ch in range(4):
            slots[pl.ds(ch, 64, stride=4), :] = turned[ch, pl.ds(hi, 64, stride=8), :]
        vals = slots[...]
        centre = jnp.sum(vals, 0, keepdims=True) * (1.0 / 256)
        off = vals - centre
        spread = jnp.sum(off * off, 0, keepdims=True) * (1.0 / 256)
        normed.append((off * lax.rsqrt(spread + 1e-05) * gain_ref[...]).astype(BF16).T)
    normed = jnp.concatenate(normed, 0)
    all_in = jnp.concatenate([ref[...] for ref in refs[0:8:2]], 0)
    all_out = jnp.concatenate([ref[...] for ref in refs[1:8:2]], 0)
    hidden = jnp.maximum(dot(normed, all_in, NT), 0.0).astype(BF16)
    total = dot(hidden, all_out, NN)
    for block in range(64):
        rows = total[block * 16 : (block + 1) * 16]
        full[block * 34 : block * 34 + 16, :] = rows[:, :128]
        full[block * 34 + 16 : block * 34 + 32, :] = rows[:, 128:]
    scores = dot(normed, gate_ref[...], NT)
    own_lanes = lax.broadcasted_iota(jnp.int32, (1024, 128), 1) // 16 == (
        lax.broadcasted_iota(jnp.int32, (1024, 128), 0) % 8
    )
    row = lax.broadcasted_iota(jnp.int32, (128, 1024), 0)
    gather = lax.broadcasted_iota(jnp.int32, (128, 1024), 1) // 8 == row % 64 * 2 + row // 64
    packed = dot(
        jnp.where(gather, 1.0, 0.0).astype(BF16), jnp.where(own_lanes, scores, 0.0).astype(BF16), NN
    )
    for half in range(2):
        full[pl.ds(32 + half, 64, stride=34), :] = packed[half * 64 : (half + 1) * 64]
    out_ref[...] = full[...].astype(BF16)


def take_kernel(
    after_ref, index_ref, table_ref, slot_ref, take_ref, score_ref, lanes_ref, bias_ref
):
    slot = slot_ref[0:1, :]
    expert = jnp.floor(slot * (1.0 / CAP))
    rank = slot - CAP * expert
    half = jnp.where(rank >= CAP // 2, 1.0, 0.0)
    codes = [rank * 64 + expert, half * 64 + expert, rank - CAP // 2 * half]
    codes = jnp.concatenate(codes + [jnp.zeros((125, 512), F32)], 0).T.astype(jnp.int32)
    take_ref[...] = (
        lax.broadcasted_iota(jnp.int32, (512, EXPERTS * CAP), 1) == codes[:, 0:1]
    ).astype(F32).astype(BF16)
    lane = lax.broadcasted_iota(jnp.int32, (512, 128), 1)
    score_ref[...] = (lane == codes[:, 1:2]).astype(F32).astype(BF16)
    lanes_ref[...] = (lane // 16 == codes[:, 2:3]).astype(F32)
    rows = []
    for t in range(TASKS):
        idx = index_ref[t : t + 1, :]
        bias = jnp.zeros((1, 512), F32)
        for r in range(table_ref.shape[1]):
            bias = jnp.where(idx == r, table_ref[t, r], bias)
        rows.append(bias)
    rows.append(jnp.zeros((128 - TASKS, 512), F32))
    bias_ref[...] = jnp.concatenate(rows, 0).T


def final_kernel(slots_ref, take_ref, score_ref, lanes_ref, bias_ref, out_ref, wide):
    wide[...] = slots_ref[...].astype(F32)

    def rows_of(at, count):
        return jnp.concatenate(
            [wide[pl.ds(at + r, 64, stride=34), :] for r in range(count)], 0
        ).astype(BF16)

    gates = dot(score_ref[...], rows_of(32, 2), NN) * lanes_ref[...]
    for shift in (64, 32, 16):
        gates = gates + pltpu.roll(gates, shift, 1)
    gates = jax.nn.sigmoid(gates + bias_ref[...])
    rows = dot(take_ref[...], jnp.concatenate([rows_of(0, 16), rows_of(16, 16)], 1), NN)
    for t in range(TASKS):
        out_ref[t] = (gates[:, t : t + 1] * rows).astype(BF16)


def call(kernel, outs, *args, scratch=(), smem=(), far=(), flops=0, vmem=32, name=None):
    specs = [
        pl.BlockSpec(memory_space=pltpu.SMEM if i in smem else pl.ANY if i in far else pltpu.VMEM)
        for i in range(len(args))
    ]
    many = isinstance(outs, (tuple, list))
    return pl.pallas_call(
        kernel,
        out_shape=outs,
        in_specs=specs,
        out_specs=[pl.BlockSpec(memory_space=pltpu.VMEM)] * len(outs)
        if many
        else pl.BlockSpec(memory_space=pltpu.VMEM),
        scratch_shapes=list(scratch),
        compiler_params=pltpu.CompilerParams(vmem_limit_bytes=vmem * 2**20),
        cost_estimate=pl.CostEstimate(flops=flops, bytes_accessed=2**20, transcendentals=0),
        name=name,
    )(*args)


def shape(dims, dtype):
    return jax.ShapeDtypeStruct(dims, dtype)


def swap(values, rows):
    lanes = values.shape[-1]
    chunks = values.reshape(64, rows, lanes)
    return lax.all_to_all(chunks, "seq", split_axis=0, concat_axis=0, tiled=True).reshape(
        64 * rows, lanes
    )


def on_device(
    events, spectral_filter, ln_gain, w_in, w_out, gate_weight, gate_table, routes, gate_index
):
    big = pltpu.VMEM
    chunks, slot = call(
        prep_kernel, [shape((1536, 128), BF16), shape((8, 512), F32)],
        events.reshape(512, 256), routes.reshape(1, 512), far=(0, 1), name="prep", vmem=60,
        scratch=[
            big((512, 256), BF16), big((1, 512), jnp.int32), big((512, 512), BF16),
            big((256, 128), F32),
            big((1536, 128), F32), pltpu.SemaphoreType.DMA((5,)),
        ],
    )
    arrived = swap(chunks, 24)
    ahead, behind = [(i, (i + 1) % 4) for i in range(4)], [(i, (i + 3) % 4) for i in range(4)]
    own_in, own_out = w_in[0], w_out[0]
    one_in = lax.ppermute(own_in, "batch", ahead)
    two_out = lax.ppermute(own_out, "batch", behind)
    far_in = lax.ppermute(one_in, "batch", ahead)
    far_out = lax.ppermute(two_out, "batch", behind)
    one_out = lax.ppermute(own_out, "batch", ahead)
    two_in = lax.ppermute(own_in, "batch", behind)
    spec = spectral_filter.reshape(2, 256, 128, 4).transpose(0, 1, 3, 2).reshape(2, 1024, 128)
    factors, turns, lanes = [jnp.asarray(t) for t in tables()]
    spec, factors, turns = call(
        ready_kernel,
        [shape((2, 128, 1024), F32), shape(factors.shape, BF16), shape(turns.shape, F32)],
        chunks, spec, factors, turns, far=(0, 1, 2, 3), name="ready",
        scratch=[big((2, 1024, 128), F32), pltpu.SemaphoreType.DMA((3,))], flops=2 * 10**9,
    )
    sums = call(
        filter_kernel, shape((512, 512), BF16), arrived, spec, factors, turns,
        scratch=[big((1536, 128), F32), big((4, 256, 128), F32), big((4, 512, 128), F32)],
        name="filter", flops=2 * 10**9,
    )
    slots_in = swap(sums, 8)
    me = lax.axis_index("seq")
    gate = lax.dynamic_index_in_dim(gate_weight.transpose(0, 2, 1), me, 1, keepdims=False)
    gate = jnp.tile(jnp.pad(gate, ((0, 16 - TASKS), (0, 0))), (8, 1))
    slots_out = call(
        expert_kernel, shape((64 * 34, 128), BF16),
        slots_in, lanes, ln_gain.reshape(256, 1), gate,
        own_in, own_out, one_in, one_out, two_in, two_out, far_in, far_out,
        name="expert", flops=10**9,
        scratch=[big((4, 512, 128), F32), big((256, 128), F32), big((64 * 34, 128), F32)],
    )
    results = lax.all_to_all(
        slots_out.reshape(64, 17, 2, 128), "seq", split_axis=0, concat_axis=0, tiled=True
    ).reshape(64 * 34, 128)
    take, score, score_lanes, bias = call(
        take_kernel,
        [
            shape((512, 1024), BF16), shape((512, 128), BF16), shape((512, 128), F32),
            shape((512, 128), F32),
        ],
        slots_out, gate_index.reshape(512, 3).T, gate_table, slot, far=(0,), smem=(2,),
        name="take", flops=2 * 10**9,
    )
    out = call(
        final_kernel, shape((3, 512, 256), BF16), results, take, score, score_lanes, bias,
        scratch=[big((64 * 34, 128), F32)], name="final",
    )
    return out.reshape(TASKS, 1, 512, 1, 256)


def solution(mesh):
    in_specs = (
        P("batch", "seq", None, None),
        P(None, None, "seq"),
        P(),
        P("seq", "batch", None),
        P("seq", "batch", None),
        P(),
        P(),
        P("batch", "seq", None, None),
        P("batch", "seq", None, None),
    )
    out_specs = P(None, "batch", "seq", None, None)
    return jax.shard_map(
        on_device, mesh=mesh, in_specs=in_specs, out_specs=out_specs, check_vma=False
    )
```

```python
import functools

import jax
import jax.numpy as jnp
import ml_dtypes
import numpy as np
from jax import lax
from jax.experimental import pallas as pl
from jax.experimental.pallas import tpu as pltpu
from jax.sharding import PartitionSpec as P

EXPERTS = 64
TASKS = 3
CAP = 16
ROWS = 256
COLS = 128
LENGTH = ROWS * COLS
BF16 = jnp.bfloat16
F32 = jnp.float32

NN = (((1,), (0,)), ((), ()))
NT = (((1,), (1,)), ((), ()))


def dot(a, b, dims):
    return lax.dot_general(a, b, dims, preferred_element_type=F32)


def split(x):
    hi = x.astype(BF16)
    return hi, (x - hi.astype(F32)).astype(BF16)


def np_split(x):
    hi = x.astype(ml_dtypes.bfloat16)
    return hi, (x - hi.astype(np.float64)).astype(ml_dtypes.bfloat16)


def cos_sin(rows, cols, points):
    angle = 2.0 * np.pi * (np.outer(np.arange(rows), np.arange(cols)) % points) / points
    return np.cos(angle), np.sin(angle)


def tables():
    cos_r, sin_r = cos_sin(ROWS, ROWS, ROWS)
    cos_c, sin_c = cos_sin(COLS, COLS, COLS)
    tw_cos, tw_sin = cos_sin(ROWS, COLS, LENGTH)
    first = np.concatenate([cos_r, -sin_r], 0)
    second = np.block([[cos_c, sin_c], [-sin_c, cos_c]])
    factors = np.concatenate([part for m in (first, second) for part in np_split(m)])
    turns = [t[i : i + 128] for t in (tw_cos, tw_sin) for i in (0, 128)]
    lane = np.arange(512)
    source = (lane // 16 % 8) * 64 + (lane // 128) * 16 + lane % 16
    lanes = (lane[:, None] == source[None, :]).astype(ml_dtypes.bfloat16)
    return factors, np.stack(turns).astype(np.float32), lanes


def prep_kernel(ev_ref, routes_ref, out_ref, slot_ref, landed, named, before, mid, wide, sems):
    copies = [
        pltpu.make_async_copy(
            ev_ref.at[pl.ds(pb * 128, 128)], landed.at[pl.ds(pb * 128, 128)], sems.at[pb]
        )
        for pb in range(4)
    ]
    copies.append(pltpu.make_async_copy(routes_ref, named, sems.at[4]))
    for copy in copies[::-1]:
        copy.start()
    before[...] = (
        lax.broadcasted_iota(jnp.int32, (512, 512), 0)
        < lax.broadcasted_iota(jnp.int32, (512, 512), 1)
    ).astype(F32).astype(BF16)
    copies[4].wait()
    experts = named[...]
    onehot = (lax.broadcasted_iota(jnp.int32, (EXPERTS, 512), 0) == experts).astype(F32)
    earlier = dot(onehot.astype(BF16), before[...], NN)
    rank = jnp.sum(earlier * onehot, 0, keepdims=True)
    experts = experts.astype(F32)
    slot_ref[...] = jnp.broadcast_to(experts * CAP + rank, (8, 512))
    for pb in range(4):
        for i, row in enumerate((experts, rank)):
            wide[pl.ds(16 + i * 4 + pb, 64, stride=24), :] = jnp.broadcast_to(
                row[:, pb * 128 : (pb + 1) * 128], (64, 128)
            )
    for pb in range(4):
        copies[pb].wait()
        mid[...] = landed[pb * 128 : (pb + 1) * 128, :].T.astype(F32)
        for ch in range(4):
            chp, chl = ch // 2, ch % 2
            wide[pl.ds(chl * 8 + pb * 2 + chp, 64, stride=24), :] = mid[pl.ds(ch, 64, stride=4), :]
    out_ref[...] = wide[...].astype(BF16)


def filter_kernel(x_ref, spec_ref, factor_ref, turn_ref, out_ref, wide, sums, stage):
    first = factor_ref[0:512], factor_ref[512:1024]
    second = factor_ref[1024:1280], factor_ref[1280:1536]
    fourth = [jnp.concatenate([part[:256], part[256:]], 1) for part in first]
    wide[...] = x_ref[...].astype(F32)
    for ch in range(4):
        for pb in range(4):
            sums[ch, pl.ds(pb, 64, stride=4), :] = wide[
                pl.ds(ch % 2 * 8 + pb * 2 + ch // 2, 64, stride=24), :
            ]
    sig = jnp.concatenate([sums[ch] for ch in range(4)], 1)
    sig16 = sig.astype(BF16)
    spec1 = dot(first[0], sig16, NN) + dot(first[1], sig16, NN)
    tcos, tsin = [jnp.concatenate([turn_ref[i], turn_ref[i + 1]], 0) for i in (0, 2)]
    turned = []
    for ch in range(4):
        re = spec1[:256, ch * 128 : (ch + 1) * 128]
        im = spec1[256:, ch * 128 : (ch + 1) * 128]
        turned.append(jnp.concatenate([re * tcos + im * tsin, im * tcos - re * tsin], 1))
    t_hi, t_lo = split(jnp.concatenate(turned, 0))
    spec2 = (
        dot(second[0], t_hi, NT) + dot(second[0], t_lo, NT) + dot(second[1], t_hi, NT)
    )
    prods = []
    for ch in range(4):
        fr = spec_ref[0, :, ch * 256 : (ch + 1) * 256]
        fi = spec_ref[1, :, ch * 256 : (ch + 1) * 256]
        zr = spec2[:128, ch * 256 : (ch + 1) * 256]
        zi = spec2[128:, ch * 256 : (ch + 1) * 256]
        prods.append(jnp.concatenate([zr * fi + zi * fr, zr * fr - zi * fi], 0))
    p_hi, p_lo = split(jnp.concatenate(prods, 1))
    back = dot(second[0], p_hi, NN) + dot(second[0], p_lo, NN) + dot(second[1], p_hi, NN)
    bcos, bsin = [jnp.concatenate([turn_ref[i].T, turn_ref[i + 1].T], 1) for i in (0, 2)]
    turned = []
    for ch in range(4):
        im = back[:128, ch * 256 : (ch + 1) * 256]
        re = back[128:, ch * 256 : (ch + 1) * 256]
        turned.append(jnp.concatenate([re * bcos - im * bsin, im * bcos + re * bsin], 1))
    v_hi, v_lo = split(jnp.concatenate(turned, 0))
    filtered = (
        dot(fourth[0], v_hi, NT) + dot(fourth[0], v_lo, NT) + dot(fourth[1], v_hi, NT)
    )
    summed = sig + filtered * (1.0 / LENGTH)
    for ch in range(4):
        sums[ch] = summed[:, ch * 128 : (ch + 1) * 128]
    low = lax.broadcasted_iota(jnp.int32, (8, 512), 0).astype(F32)

    def spread(ref_rows):
        return jnp.concatenate([jnp.broadcast_to(r, (8, 128)) for r in ref_rows], 1)

    def place(block):
        at = block * 24 + 16
        expert = spread([wide[pl.ds(at + pb, 1), :] for pb in range(4)])
        rank = spread([wide[pl.ds(at + 4 + pb, 1), :] for pb in range(4)])
        to = jnp.concatenate(
            [jnp.where(expert == low + 8.0 * m, 1.0, 0.0) for m in range(8)], 0
        ).astype(BF16)
        here = [rank == low, rank == low + 8.0]
        values = []
        for ch in range(4):
            vals = spread([sums[ch, pl.ds(block * 4 + pb, 1), :] for pb in range(4)])
            values += [jnp.where(m, vals, 0.0) for m in here]
        return dot(to, jnp.concatenate(values, 0).astype(BF16), NT)

    def group(hi, carry):
        for q in range(4):
            pair = [place(hi * 8 + q * 2 + half) for half in range(2)]
            stage[q, pl.ds(hi, 64, stride=8), :] = jnp.concatenate(pair, 1)
        return carry

    lax.fori_loop(0, 8, group, 0, unroll=8)
    for q in range(4):
        out_ref[:, q * 128 : (q + 1) * 128] = stage[q].astype(BF16)


def ready_kernel(
    after_ref, spec_ref, factor_ref, turn_ref, spec_out, factor_out, turn_out, raw, sems
):
    copies = [
        pltpu.make_async_copy(src, dst, sems.at[i])
        for i, (src, dst) in enumerate(
            ((spec_ref, raw), (factor_ref, factor_out), (turn_ref, turn_out))
        )
    ]
    for copy in copies:
        copy.start()
    copies[0].wait()
    for part in range(2):
        for ch in range(4):
            for half in range(2):
                at = ch * 256 + half * 128
                spec_out[part, :, at : at + 128] = raw[part, pl.ds(4 * half + ch, 128, stride=8), :]
    copies[1].wait()
    copies[2].wait()


def expert_kernel(
    x_ref, lanes_ref, gain_ref, gate_ref, *refs
):
    out_ref, turned, slots, full = refs[8:]
    moved = dot(x_ref[...], lanes_ref[...], NN)
    for ch in range(4):
        turned[ch] = moved[:, ch * 128 : (ch + 1) * 128]
    normed = []
    for hi in range(8):
        for ch in range(4):
            slots[pl.ds(ch, 64, stride=4), :] = turned[ch, pl.ds(hi, 64, stride=8), :]
        vals = slots[...]
        centre = jnp.sum(vals, 0, keepdims=True) * (1.0 / 256)
        off = vals - centre
        spread = jnp.sum(off * off, 0, keepdims=True) * (1.0 / 256)
        normed.append((off * lax.rsqrt(spread + 1e-05) * gain_ref[...]).astype(BF16).T)
    normed = jnp.concatenate(normed, 0)
    all_in = jnp.concatenate([ref[...] for ref in refs[0:8:2]], 0)
    all_out = jnp.concatenate([ref[...] for ref in refs[1:8:2]], 0)
    hidden = jnp.maximum(dot(normed, all_in, NT), 0.0).astype(BF16)
    total = dot(hidden, all_out, NN)
    for block in range(64):
        rows = total[block * 16 : (block + 1) * 16]
        full[block * 34 : block * 34 + 16, :] = rows[:, :128]
        full[block * 34 + 16 : block * 34 + 32, :] = rows[:, 128:]
    scores = dot(normed, jnp.concatenate([gate_ref[...]] * 8, 0), NT)
    own_lanes = lax.broadcasted_iota(jnp.int32, (1024, 128), 1) // 16 == (
        lax.broadcasted_iota(jnp.int32, (1024, 128), 0) % 8
    )
    row = lax.broadcasted_iota(jnp.int32, (128, 1024), 0)
    gather = lax.broadcasted_iota(jnp.int32, (128, 1024), 1) // 8 == row % 64 * 2 + row // 64
    packed = dot(
        jnp.where(gather, 1.0, 0.0).astype(BF16), jnp.where(own_lanes, scores, 0.0).astype(BF16), NN
    )
    for half in range(2):
        full[pl.ds(32 + half, 64, stride=34), :] = packed[half * 64 : (half + 1) * 64]
    out_ref[...] = full[...].astype(BF16)


def take_kernel(
    after_ref, index_ref, table_ref, slot_ref, take_ref, score_ref, lanes_ref, bias_ref
):
    slot = slot_ref[0:1, :]
    expert = jnp.floor(slot * (1.0 / CAP))
    rank = slot - CAP * expert
    half = jnp.where(rank >= CAP // 2, 1.0, 0.0)
    codes = [rank * 64 + expert, half * 64 + expert, rank - CAP // 2 * half]
    codes = jnp.concatenate(codes + [jnp.zeros((125, 512), F32)], 0).T.astype(jnp.int32)
    take_ref[...] = (
        lax.broadcasted_iota(jnp.int32, (512, EXPERTS * CAP), 1) == codes[:, 0:1]
    ).astype(F32).astype(BF16)
    lane = lax.broadcasted_iota(jnp.int32, (512, 128), 1)
    score_ref[...] = (lane == codes[:, 1:2]).astype(F32).astype(BF16)
    lanes_ref[...] = (lane // 16 == codes[:, 2:3]).astype(F32)
    rows = []
    for t in range(TASKS):
        idx = index_ref[t : t + 1, :]
        bias = jnp.zeros((1, 512), F32)
        for r in range(table_ref.shape[1]):
            bias = jnp.where(idx == r, table_ref[t, r], bias)
        rows.append(bias)
    rows.append(jnp.zeros((128 - TASKS, 512), F32))
    bias_ref[...] = jnp.concatenate(rows, 0).T


def final_kernel(slots_ref, take_ref, score_ref, lanes_ref, bias_ref, out_ref, wide):
    wide[...] = slots_ref[...].astype(F32)

    def rows_of(at, count):
        return jnp.concatenate(
            [wide[pl.ds(at + r, 64, stride=34), :] for r in range(count)], 0
        ).astype(BF16)

    gates = dot(score_ref[...], rows_of(32, 2), NN) * lanes_ref[...]
    for shift in (64, 32, 16):
        gates = gates + pltpu.roll(gates, shift, 1)
    gates = jax.nn.sigmoid(gates + bias_ref[...])
    rows = dot(take_ref[...], jnp.concatenate([rows_of(0, 16), rows_of(16, 16)], 1), NN)
    for t in range(TASKS):
        out_ref[t] = (gates[:, t : t + 1] * rows).astype(BF16)


def call(kernel, outs, *args, scratch=(), smem=(), far=(), flops=0, vmem=32, name=None):
    specs = [
        pl.BlockSpec(memory_space=pltpu.SMEM if i in smem else pl.ANY if i in far else pltpu.VMEM)
        for i in range(len(args))
    ]
    many = isinstance(outs, (tuple, list))
    return pl.pallas_call(
        kernel,
        out_shape=outs,
        in_specs=specs,
        out_specs=[pl.BlockSpec(memory_space=pltpu.VMEM)] * len(outs)
        if many
        else pl.BlockSpec(memory_space=pltpu.VMEM),
        scratch_shapes=list(scratch),
        compiler_params=pltpu.CompilerParams(vmem_limit_bytes=vmem * 2**20),
        cost_estimate=pl.CostEstimate(flops=flops, bytes_accessed=2**20, transcendentals=0),
        name=name,
    )(*args)


def shape(dims, dtype):
    return jax.ShapeDtypeStruct(dims, dtype)


def swap(values, rows):
    lanes = values.shape[-1]
    chunks = values.reshape(64, rows, lanes)
    return lax.all_to_all(chunks, "seq", split_axis=0, concat_axis=0, tiled=True).reshape(
        64 * rows, lanes
    )


def on_device(
    events, spectral_filter, ln_gain, w_in, w_out, gate_weight, gate_table, routes, gate_index
):
    big = pltpu.VMEM
    chunks, slot = call(
        prep_kernel, [shape((1536, 128), BF16), shape((8, 512), F32)],
        events.reshape(512, 256), routes.reshape(1, 512), far=(0, 1), name="prep", vmem=60,
        scratch=[
            big((512, 256), BF16), big((1, 512), jnp.int32), big((512, 512), BF16),
            big((256, 128), F32),
            big((1536, 128), F32), pltpu.SemaphoreType.DMA((5,)),
        ],
    )
    arrived = swap(chunks, 24)
    ahead, behind = [(i, (i + 1) % 4) for i in range(4)], [(i, (i + 3) % 4) for i in range(4)]
    own_in, own_out = w_in[0], w_out[0]
    one_in = lax.ppermute(own_in, "batch", ahead)
    two_out = lax.ppermute(own_out, "batch", behind)
    far_in = lax.ppermute(one_in, "batch", ahead)
    far_out = lax.ppermute(two_out, "batch", behind)
    one_out = lax.ppermute(own_out, "batch", ahead)
    two_in = lax.ppermute(own_in, "batch", behind)
    spec = spectral_filter.reshape(2, 256, 128, 4).transpose(0, 1, 3, 2).reshape(2, 1024, 128)
    factors, turns, lanes = [jnp.asarray(t) for t in tables()]
    spec, factors, turns = call(
        ready_kernel,
        [shape((2, 128, 1024), F32), shape(factors.shape, BF16), shape(turns.shape, F32)],
        chunks, spec, factors, turns, far=(0, 1, 2, 3), name="ready",
        scratch=[big((2, 1024, 128), F32), pltpu.SemaphoreType.DMA((3,))], flops=2 * 10**9,
    )
    sums = call(
        filter_kernel, shape((512, 512), BF16), arrived, spec, factors, turns,
        scratch=[big((1536, 128), F32), big((4, 256, 128), F32), big((4, 512, 128), F32)],
        name="filter", flops=2 * 10**9,
    )
    slots_in = swap(sums, 8)
    me = lax.axis_index("seq")
    gate = lax.dynamic_index_in_dim(gate_weight.transpose(0, 2, 1), me, 1, keepdims=False)
    gate = jnp.pad(gate, ((0, 16 - TASKS), (0, 0)))
    slots_out = call(
        expert_kernel, shape((64 * 34, 128), BF16),
        slots_in, lanes, ln_gain.reshape(256, 1), gate,
        own_in, own_out, one_in, one_out, two_in, two_out, far_in, far_out,
        name="expert", flops=10**9,
        scratch=[big((4, 512, 128), F32), big((256, 128), F32), big((64 * 34, 128), F32)],
    )
    results = lax.all_to_all(
        slots_out.reshape(64, 17, 2, 128), "seq", split_axis=0, concat_axis=0, tiled=True
    ).reshape(64 * 34, 128)
    take, score, score_lanes, bias = call(
        take_kernel,
        [
            shape((512, 1024), BF16), shape((512, 128), BF16), shape((512, 128), F32),
            shape((512, 128), F32),
        ],
        slots_out, gate_index.reshape(512, 3).T, gate_table, slot, far=(0,), smem=(2,),
        name="take", flops=2 * 10**9,
    )
    out = call(
        final_kernel, shape((3, 512, 256), BF16), results, take, score, score_lanes, bias,
        scratch=[big((64 * 34, 128), F32)], name="final",
    )
    return out.reshape(TASKS, 1, 512, 1, 256)


def solution(mesh):
    in_specs = (
        P("batch", "seq", None, None),
        P(None, None, "seq"),
        P(),
        P("seq", "batch", None),
        P("seq", "batch", None),
        P(),
        P(),
        P("batch", "seq", None, None),
        P("batch", "seq", None, None),
    )
    out_specs = P(None, "batch", "seq", None, None)
    return jax.shard_map(
        on_device, mesh=mesh, in_specs=in_specs, out_specs=out_specs, check_vma=False
    )
```

```python
import functools

import jax
import jax.numpy as jnp
import ml_dtypes
import numpy as np
from jax import lax
from jax.experimental import pallas as pl
from jax.experimental.pallas import tpu as pltpu
from jax.sharding import PartitionSpec as P

EXPERTS = 64
TASKS = 3
CAP = 16
ROWS = 256
COLS = 128
LENGTH = ROWS * COLS
BF16 = jnp.bfloat16
F32 = jnp.float32

NN = (((1,), (0,)), ((), ()))
NT = (((1,), (1,)), ((), ()))


def dot(a, b, dims):
    return lax.dot_general(a, b, dims, preferred_element_type=F32)


def split(x):
    hi = x.astype(BF16)
    return hi, (x - hi.astype(F32)).astype(BF16)


def np_split(x):
    hi = x.astype(ml_dtypes.bfloat16)
    return hi, (x - hi.astype(np.float64)).astype(ml_dtypes.bfloat16)


def cos_sin(rows, cols, points):
    angle = 2.0 * np.pi * (np.outer(np.arange(rows), np.arange(cols)) % points) / points
    return np.cos(angle), np.sin(angle)


def tables():
    cos_r, sin_r = cos_sin(ROWS, ROWS, ROWS)
    cos_c, sin_c = cos_sin(COLS, COLS, COLS)
    tw_cos, tw_sin = cos_sin(ROWS, COLS, LENGTH)
    first = np.concatenate([cos_r, -sin_r], 0)
    second = np.block([[cos_c, sin_c], [-sin_c, cos_c]])
    factors = np.concatenate([part for m in (first, second) for part in np_split(m)])
    turns = [t[i : i + 128] for t in (tw_cos, tw_sin) for i in (0, 128)]
    lane = np.arange(512)
    source = (lane // 16 % 8) * 64 + (lane // 128) * 16 + lane % 16
    lanes = (lane[:, None] == source[None, :]).astype(ml_dtypes.bfloat16)
    return factors, np.stack(turns).astype(np.float32), lanes


def prep_kernel(ev_ref, routes_ref, out_ref, slot_ref, landed, named, before, mid, wide, sems):
    copies = [
        pltpu.make_async_copy(
            ev_ref.at[pl.ds(pb * 128, 128)], landed.at[pl.ds(pb * 128, 128)], sems.at[pb]
        )
        for pb in range(4)
    ]
    copies.append(pltpu.make_async_copy(routes_ref, named, sems.at[4]))
    for copy in copies[::-1]:
        copy.start()
    before[...] = (
        lax.broadcasted_iota(jnp.int32, (512, 512), 0)
        < lax.broadcasted_iota(jnp.int32, (512, 512), 1)
    ).astype(F32).astype(BF16)
    copies[4].wait()
    experts = named[...]
    onehot = (lax.broadcasted_iota(jnp.int32, (EXPERTS, 512), 0) == experts).astype(F32)
    earlier = dot(onehot.astype(BF16), before[...], NN)
    rank = jnp.sum(earlier * onehot, 0, keepdims=True)
    experts = experts.astype(F32)
    slot_ref[...] = jnp.broadcast_to(experts * CAP + rank, (8, 512))
    for pb in range(4):
        for i, row in enumerate((experts, rank)):
            wide[pl.ds(16 + i * 4 + pb, 64, stride=24), :] = jnp.broadcast_to(
                row[:, pb * 128 : (pb + 1) * 128], (64, 128)
            )
    for pb in range(4):
        copies[pb].wait()
        mid[...] = landed[pb * 128 : (pb + 1) * 128, :].T.astype(F32)
        for ch in range(4):
            chp, chl = ch // 2, ch % 2
            wide[pl.ds(chl * 8 + pb * 2 + chp, 64, stride=24), :] = mid[pl.ds(ch, 64, stride=4), :]
    out_ref[...] = wide[...].astype(BF16)


def filter_kernel(x_ref, spec_ref, factor_ref, turn_ref, out_ref, wide, sums, stage):
    first = factor_ref[0:512], factor_ref[512:1024]
    second = factor_ref[1024:1280], factor_ref[1280:1536]
    fourth = [jnp.concatenate([part[:256], part[256:]], 1) for part in first]
    wide[...] = x_ref[...].astype(F32)
    for ch in range(4):
        for pb in range(4):
            sums[ch, pl.ds(pb, 64, stride=4), :] = wide[
                pl.ds(ch % 2 * 8 + pb * 2 + ch // 2, 64, stride=24), :
            ]
    sig = jnp.concatenate([sums[ch] for ch in range(4)], 1)
    sig16 = sig.astype(BF16)
    spec1 = dot(first[0], sig16, NN) + dot(first[1], sig16, NN)
    tcos, tsin = [jnp.concatenate([turn_ref[i], turn_ref[i + 1]], 0) for i in (0, 2)]
    turned = []
    for ch in range(4):
        re = spec1[:256, ch * 128 : (ch + 1) * 128]
        im = spec1[256:, ch * 128 : (ch + 1) * 128]
        turned.append(jnp.concatenate([re * tcos + im * tsin, im * tcos - re * tsin], 1))
    t_hi, t_lo = split(jnp.concatenate(turned, 0))
    spec2 = (
        dot(second[0], t_hi, NT) + dot(second[0], t_lo, NT) + dot(second[1], t_hi, NT)
    )
    prods = []
    for ch in range(4):
        fr = spec_ref[0, :, ch * 256 : (ch + 1) * 256]
        fi = spec_ref[1, :, ch * 256 : (ch + 1) * 256]
        zr = spec2[:128, ch * 256 : (ch + 1) * 256]
        zi = spec2[128:, ch * 256 : (ch + 1) * 256]
        prods.append(jnp.concatenate([zr * fi + zi * fr, zr * fr - zi * fi], 0))
    p_hi, p_lo = split(jnp.concatenate(prods, 1))
    back = dot(second[0], p_hi, NN) + dot(second[0], p_lo, NN) + dot(second[1], p_hi, NN)
    bcos, bsin = [jnp.concatenate([turn_ref[i].T, turn_ref[i + 1].T], 1) for i in (0, 2)]
    turned = []
    for ch in range(4):
        im = back[:128, ch * 256 : (ch + 1) * 256]
        re = back[128:, ch * 256 : (ch + 1) * 256]
        turned.append(jnp.concatenate([re * bcos - im * bsin, im * bcos + re * bsin], 1))
    v_hi, v_lo = split(jnp.concatenate(turned, 0))
    filtered = (
        dot(fourth[0], v_hi, NT) + dot(fourth[0], v_lo, NT) + dot(fourth[1], v_hi, NT)
    )
    summed = sig + filtered * (1.0 / LENGTH)
    for ch in range(4):
        sums[ch] = summed[:, ch * 128 : (ch + 1) * 128]
    low = lax.broadcasted_iota(jnp.int32, (8, 512), 0).astype(F32)

    def spread(ref_rows):
        return jnp.concatenate([jnp.broadcast_to(r, (8, 128)) for r in ref_rows], 1)

    def place(block):
        at = block * 24 + 16
        expert = spread([wide[pl.ds(at + pb, 1), :] for pb in range(4)])
        rank = spread([wide[pl.ds(at + 4 + pb, 1), :] for pb in range(4)])
        to = jnp.concatenate(
            [jnp.where(expert == low + 8.0 * m, 1.0, 0.0) for m in range(8)], 0
        ).astype(BF16)
        here = [rank == low, rank == low + 8.0]
        values = []
        for ch in range(4):
            vals = spread([sums[ch, pl.ds(block * 4 + pb, 1), :] for pb in range(4)])
            values += [jnp.where(m, vals, 0.0) for m in here]
        return dot(to, jnp.concatenate(values, 0).astype(BF16), NT)

    def group(hi, carry):
        for q in range(4):
            pair = [place(hi * 8 + q * 2 + half) for half in range(2)]
            stage[q, pl.ds(hi, 64, stride=8), :] = jnp.concatenate(pair, 1)
        return carry

    lax.fori_loop(0, 8, group, 0, unroll=8)
    for q in range(4):
        out_ref[:, q * 128 : (q + 1) * 128] = stage[q].astype(BF16)


def ready_kernel(
    after_ref, spec_ref, factor_ref, turn_ref, spec_out, factor_out, turn_out, raw, sems
):
    copies = [
        pltpu.make_async_copy(src, dst, sems.at[i])
        for i, (src, dst) in enumerate(
            ((spec_ref, raw), (factor_ref, factor_out), (turn_ref, turn_out))
        )
    ]
    for copy in copies:
        copy.start()
    copies[0].wait()
    for part in range(2):
        for ch in range(4):
            for half in range(2):
                at = ch * 256 + half * 128
                spec_out[part, :, at : at + 128] = raw[part, pl.ds(4 * half + ch, 128, stride=8), :]
    copies[1].wait()
    copies[2].wait()


def expert_kernel(
    x_ref, lanes_ref, gain_ref, gate_ref, *refs
):
    out_ref, turned, slots, full = refs[8:]
    moved = dot(x_ref[...], lanes_ref[...], NN)
    for ch in range(4):
        turned[ch] = moved[:, ch * 128 : (ch + 1) * 128]
    normed = []
    for hi in range(8):
        for ch in range(4):
            slots[pl.ds(ch, 64, stride=4), :] = turned[ch, pl.ds(hi, 64, stride=8), :]
        vals = slots[...]
        centre = jnp.sum(vals, 0, keepdims=True) * (1.0 / 256)
        off = vals - centre
        spread = jnp.sum(off * off, 0, keepdims=True) * (1.0 / 256)
        normed.append((off * lax.rsqrt(spread + 1e-05) * gain_ref[...]).astype(BF16).T)
    normed = jnp.concatenate(normed, 0)
    all_in = jnp.concatenate([ref[...] for ref in refs[0:8:2]], 0)
    all_out = jnp.concatenate([ref[...] for ref in refs[1:8:2]], 0)
    hidden = jnp.maximum(dot(normed, all_in, NT), 0.0).astype(BF16)
    total = dot(hidden, all_out, NN)
    for block in range(64):
        rows = total[block * 16 : (block + 1) * 16]
        full[block * 34 : block * 34 + 16, :] = rows[:, :128]
        full[block * 34 + 16 : block * 34 + 32, :] = rows[:, 128:]
    scores = dot(normed, jnp.concatenate([gate_ref[...]] * 8, 0), NT)
    own_lanes = lax.broadcasted_iota(jnp.int32, (1024, 128), 1) // 16 == (
        lax.broadcasted_iota(jnp.int32, (1024, 128), 0) % 8
    )
    row = lax.broadcasted_iota(jnp.int32, (128, 1024), 0)
    gather = lax.broadcasted_iota(jnp.int32, (128, 1024), 1) // 8 == row % 64 * 2 + row // 64
    packed = dot(
        jnp.where(gather, 1.0, 0.0).astype(BF16), jnp.where(own_lanes, scores, 0.0).astype(BF16), NN
    )
    for half in range(2):
        full[pl.ds(32 + half, 64, stride=34), :] = packed[half * 64 : (half + 1) * 64]
    out_ref[...] = full[...].astype(BF16)


def take_kernel(
    after_ref, index_ref, table_ref, slot_ref, take_ref, score_ref, lanes_ref, bias_ref
):
    slot = slot_ref[0:1, :]
    expert = jnp.floor(slot * (1.0 / CAP))
    rank = slot - CAP * expert
    half = jnp.where(rank >= CAP // 2, 1.0, 0.0)
    codes = [rank * 64 + expert, half * 64 + expert, rank - CAP // 2 * half]
    codes = jnp.concatenate(codes + [jnp.zeros((125, 512), F32)], 0).T.astype(jnp.int32)
    take_ref[...] = (
        lax.broadcasted_iota(jnp.int32, (512, EXPERTS * CAP), 1) == codes[:, 0:1]
    ).astype(F32).astype(BF16)
    lane = lax.broadcasted_iota(jnp.int32, (512, 128), 1)
    score_ref[...] = (lane == codes[:, 1:2]).astype(F32).astype(BF16)
    lanes_ref[...] = (lane // 16 == codes[:, 2:3]).astype(F32)
    rows = []
    for t in range(TASKS):
        idx = index_ref[t : t + 1, :]
        bias = jnp.zeros((1, 512), F32)
        for r in range(table_ref.shape[1]):
            bias = jnp.where(idx == r, table_ref[t, r], bias)
        rows.append(bias)
    rows.append(jnp.zeros((128 - TASKS, 512), F32))
    bias_ref[...] = jnp.concatenate(rows, 0).T


def final_kernel(slots_ref, take_ref, score_ref, lanes_ref, bias_ref, out_ref, wide):
    wide[...] = slots_ref[...].astype(F32)

    def rows_of(at, count):
        return jnp.concatenate(
            [wide[pl.ds(at + r, 64, stride=34), :] for r in range(count)], 0
        ).astype(BF16)

    gates = dot(score_ref[...], rows_of(32, 2), NN) * lanes_ref[...]
    for shift in (64, 32, 16):
        gates = gates + pltpu.roll(gates, shift, 1)
    gates = jax.nn.sigmoid(gates + bias_ref[...])
    rows = dot(take_ref[...], jnp.concatenate([rows_of(0, 16), rows_of(16, 16)], 1), NN)
    for t in range(TASKS):
        out_ref[t] = (gates[:, t : t + 1] * rows).astype(BF16)


def call(kernel, outs, *args, scratch=(), smem=(), far=(), flops=0, vmem=32, name=None):
    specs = [
        pl.BlockSpec(memory_space=pltpu.SMEM if i in smem else pl.ANY if i in far else pltpu.VMEM)
        for i in range(len(args))
    ]
    many = isinstance(outs, (tuple, list))
    return pl.pallas_call(
        kernel,
        out_shape=outs,
        in_specs=specs,
        out_specs=[pl.BlockSpec(memory_space=pltpu.VMEM)] * len(outs)
        if many
        else pl.BlockSpec(memory_space=pltpu.VMEM),
        scratch_shapes=list(scratch),
        compiler_params=pltpu.CompilerParams(vmem_limit_bytes=vmem * 2**20),
        cost_estimate=pl.CostEstimate(flops=flops, bytes_accessed=2**20, transcendentals=0),
        name=name,
    )(*args)


def shape(dims, dtype):
    return jax.ShapeDtypeStruct(dims, dtype)


def swap(values, rows):
    lanes = values.shape[-1]
    chunks = values.reshape(64, rows, lanes)
    return lax.all_to_all(chunks, "seq", split_axis=0, concat_axis=0, tiled=True).reshape(
        64 * rows, lanes
    )


def on_device(
    events, spectral_filter, ln_gain, w_in, w_out, gate_weight, gate_table, routes, gate_index
):
    big = pltpu.VMEM
    chunks, slot = call(
        prep_kernel, [shape((1536, 128), BF16), shape((8, 512), F32)],
        events.reshape(512, 256), routes.reshape(1, 512), far=(0, 1), name="prep", vmem=60,
        scratch=[
            big((512, 256), BF16), big((1, 512), jnp.int32), big((512, 512), BF16),
            big((256, 128), F32),
            big((1536, 128), F32), pltpu.SemaphoreType.DMA((5,)),
        ],
    )
    arrived = swap(chunks, 24)
    ahead, behind = [(i, (i + 1) % 4) for i in range(4)], [(i, (i + 3) % 4) for i in range(4)]
    own_in, own_out = w_in[0], w_out[0]
    one_in = lax.ppermute(own_in, "batch", ahead)
    two_out = lax.ppermute(own_out, "batch", behind)
    far_in = lax.ppermute(one_in, "batch", ahead)
    far_out = lax.ppermute(two_out, "batch", behind)
    one_out = lax.ppermute(own_out, "batch", ahead)
    two_in = lax.ppermute(own_in, "batch", behind)
    spec = spectral_filter.reshape(2, 256, 128, 4).transpose(0, 1, 3, 2).reshape(2, 1024, 128)
    factors, turns, lanes = [jnp.asarray(t) for t in tables()]
    spec, factors, turns = call(
        ready_kernel,
        [shape((2, 128, 1024), F32), shape(factors.shape, BF16), shape(turns.shape, F32)],
        slot, spec, factors, turns, far=(0, 1, 2, 3), name="ready",
        scratch=[big((2, 1024, 128), F32), pltpu.SemaphoreType.DMA((3,))], flops=2 * 10**9,
    )
    sums = call(
        filter_kernel, shape((512, 512), BF16), arrived, spec, factors, turns,
        scratch=[big((1536, 128), F32), big((4, 256, 128), F32), big((4, 512, 128), F32)],
        name="filter", flops=2 * 10**9,
    )
    slots_in = swap(sums, 8)
    me = lax.axis_index("seq")
    gate = lax.dynamic_index_in_dim(gate_weight.transpose(0, 2, 1), me, 1, keepdims=False)
    gate = jnp.pad(gate, ((0, 16 - TASKS), (0, 0)))
    slots_out = call(
        expert_kernel, shape((64 * 34, 128), BF16),
        slots_in, lanes, ln_gain.reshape(256, 1), gate,
        own_in, own_out, one_in, one_out, two_in, two_out, far_in, far_out,
        name="expert", flops=10**9,
        scratch=[big((4, 512, 128), F32), big((256, 128), F32), big((64 * 34, 128), F32)],
    )
    results = lax.all_to_all(
        slots_out.reshape(64, 17, 2, 128), "seq", split_axis=0, concat_axis=0, tiled=True
    ).reshape(64 * 34, 128)
    take, score, score_lanes, bias = call(
        take_kernel,
        [
            shape((512, 1024), BF16), shape((512, 128), BF16), shape((512, 128), F32),
            shape((512, 128), F32),
        ],
        slots_out, gate_index.reshape(512, 3).T, gate_table, slot, far=(0,), smem=(2,),
        name="take", flops=2 * 10**9,
    )
    out = call(
        final_kernel, shape((3, 512, 256), BF16), results, take, score, score_lanes, bias,
        scratch=[big((64 * 34, 128), F32)], name="final",
    )
    return out.reshape(TASKS, 1, 512, 1, 256)


def solution(mesh):
    in_specs = (
        P("batch", "seq", None, None),
        P(None, None, "seq"),
        P(),
        P("seq", "batch", None),
        P("seq", "batch", None),
        P(),
        P(),
        P("batch", "seq", None, None),
        P("batch", "seq", None, None),
    )
    out_specs = P(None, "batch", "seq", None, None)
    return jax.shard_map(
        on_device, mesh=mesh, in_specs=in_specs, out_specs=out_specs, check_vma=False
    )
```
